32 devices in a mesh: groups: 2 (over x), owner: 16 (over z, y, core), tensor: 1.
Axes of the slice: x: 2, y: 2, z: 4, core: 2. Of those that a mesh axis runs over, the one named last changes fastest.
Arguments:
- tokens: bfloat16 [6144, 4096], P(('groups', 'owner'), 'tensor'), parts along dimension 0, may hold values from -3 to 3
- cotangent: bfloat16 [6144, 1024], P(('groups', 'owner')), parts along dimension 0, may hold values from -6 to 6
- frozen_value_weight: bfloat16 [4096, 1024], P('tensor'), may hold values from -0.09375 to 0.09375
- adapter_down_weight: bfloat16 [16, 64, 4096], P('owner', None, 'tensor'), may hold values from -0.09375 to 0.09375
- adapter_up_weight: bfloat16 [16, 64, 1024], P('owner', None, 'tensor'), may hold values from -0.1875 to 0.1875
- speaker_of_clip: int32 [512], P('groups'), parts along dimension 0, may hold values from 0 to 15, as said below
Outputs:
- input_row_gradient: bfloat16 [6144, 4096], P(('groups', 'owner'), 'tensor'), parts along dimension 0
- down_grad: float32 [32, 64, 4096], P(('groups', 'owner'), None, 'tensor'), parts along dimension 0
- up_grad: float32 [32, 64, 1024], P(('groups', 'owner'), None, 'tensor'), parts along dimension 0
The draws below stay inside these ranges and needn't reach their ends.
There are 2 independent parts, one for each index of `groups`. The reference program is written for one: setup_inputs(seed, part) draws one part's arguments, and reference() takes and returns one part's arrays. A program takes and returns all parts, laid end to end along the dimension named above; an argument that names none is the same for every part. Nothing has to cross between parts.
Inputs may be any that keep to these rules, and one draw needn't show every extreme that they name: `speaker_of_clip`: the clips of one device (aligned blocks of 16 entries) name no speaker more than 2 times, and one and the same speaker is named exactly 2 times in every block of a part.
All inputs are finite; a program needn't handle non-finite values.
Results may differ from the reference program's by a relative error of at most 0.0034.
Values may be sent and summed in bfloat16 or wider, within the bound.
A program may use at most 128 MiB of HBM per device.

```python
import jax
import jax.numpy as jnp
from jax import lax

MODEL_WIDTH = 4096
VALUE_WIDTH = 1024
ADAPTER_RANK = 64
CAP = 2
CLIP_LEN = 12
CLIP_DEV = 16
CLIPS = 256
TOKEN_TOTAL = 3072
SPEAKER_COUNT = 16


def draw_speaker_of_clip(key, part):
    key = jax.random.fold_in(key, 7)
    pick_key, block_key, order_key = jax.random.split(key, 3)
    blocks = CLIPS // CLIP_DEV
    busiest = jax.random.randint(pick_key, (), 0, SPEAKER_COUNT, dtype=jnp.int32)
    others = jnp.repeat(jnp.arange(SPEAKER_COUNT - 1, dtype=jnp.int32), CAP)
    others = others + (others >= busiest).astype(jnp.int32)

    def one_block(block_seed, order_seed):
        chosen = jax.random.permutation(block_seed, others)[:CLIP_DEV - CAP]
        filled = jnp.concatenate([jnp.full((CAP,), busiest, jnp.int32), chosen])
        return jax.random.permutation(order_seed, filled)
    result = jax.vmap(one_block)(jax.random.split(block_key, blocks), jax.random.split(order_key, blocks))
    return result.reshape(-1).astype(jnp.int32)


def shard_levels(own_key, extent, pieces, least, largest):
    def one(axis_at, shards_of):
        draws = jax.random.uniform(jax.random.fold_in(jax.random.fold_in(own_key, 6), axis_at), (shards_of,), jnp.float32, least / len(pieces), largest / len(pieces))
        return jnp.repeat(jnp.exp(draws), extent[axis_at] // shards_of).reshape((-1,) + (1,) * (len(extent) - axis_at - 1))

    loudness = one(*pieces[0])
    for cut in pieces[1:]:
        loudness = loudness * one(*cut)
    return loudness


def gaussian(key, shape, scale, most, cuts=(), kind=jnp.bfloat16):
    drawn = scale * jax.random.normal(key, shape, jnp.float32)
    if cuts:
        drawn = drawn * shard_levels(key, shape, cuts, -0.22, 0.18)
    return jnp.clip(drawn, -most, most).astype(kind)


def setup_inputs(seed: int = 0, part: int = 0) -> dict:
    key_of = jax.random.split(jax.random.key(seed), 7)
    own_keys = jax.random.split(jax.random.fold_in(key_of[6], part), 7)
    tokens = gaussian(own_keys[0], (TOKEN_TOTAL, MODEL_WIDTH), 0.5, 3.0, ((0, 16),))
    cotangent = gaussian(own_keys[1], (TOKEN_TOTAL, VALUE_WIDTH), 1.0, 6.0, ((0, 16),))
    frozen_value_weight = gaussian(key_of[2], (MODEL_WIDTH, VALUE_WIDTH), MODEL_WIDTH ** -0.5, 0.09375)
    adapter_down_weight = gaussian(key_of[3], (SPEAKER_COUNT, ADAPTER_RANK, MODEL_WIDTH), MODEL_WIDTH ** -0.5, 0.09375, ((0, 16),))
    adapter_up_weight = gaussian(key_of[4], (SPEAKER_COUNT, ADAPTER_RANK, VALUE_WIDTH), VALUE_WIDTH ** -0.5, 0.1875, ((0, 16),))
    speaker_of_clip = draw_speaker_of_clip(jax.random.fold_in(jax.random.fold_in(key_of[6], part), 71), part)
    return dict(tokens=tokens, cotangent=cotangent, frozen_value_weight=frozen_value_weight, adapter_down_weight=adapter_down_weight, adapter_up_weight=adapter_up_weight, speaker_of_clip=speaker_of_clip)


def reference(tokens, cotangent, frozen_value_weight, adapter_down_weight, adapter_up_weight, speaker_of_clip):
    contract_last = (((1,), (1,)), ((), ()))
    contract_leading = (((0,), (0,)), ((), ()))
    frozen_gradient = lax.dot_general(cotangent, frozen_value_weight, contract_last, preferred_element_type=jnp.float32)
    clip_token_rows = tokens.reshape(CLIPS, CLIP_LEN, MODEL_WIDTH)
    clip_output_gradient = cotangent.reshape(CLIPS, CLIP_LEN, VALUE_WIDTH)

    def single_clip_step(carry, item):
        down_gradient_total, up_gradient_total = carry
        rows, cotan_rows, speaker_index = item
        speaker_down_factor = adapter_down_weight[speaker_index]
        speaker_up_factor = adapter_up_weight[speaker_index]
        adapter_acts = lax.dot_general(speaker_down_factor, rows, contract_last, preferred_element_type=jnp.float32)
        adapter_back = lax.dot_general(speaker_up_factor, cotan_rows, contract_last, preferred_element_type=jnp.float32)
        acts_low = adapter_acts.astype(jnp.bfloat16)
        low_rank_gradient = adapter_back.astype(jnp.bfloat16)
        down_part = jnp.dot(low_rank_gradient, rows, preferred_element_type=jnp.float32)
        up_part = jnp.dot(acts_low, cotan_rows, preferred_element_type=jnp.float32)
        adapter_low_rows = lax.dot_general(low_rank_gradient, speaker_down_factor, contract_leading, preferred_element_type=jnp.float32)
        down_gradient_total = down_gradient_total.at[speaker_index].add(down_part)
        up_gradient_total = up_gradient_total.at[speaker_index].add(up_part)
        return (down_gradient_total, up_gradient_total), adapter_low_rows.astype(jnp.bfloat16)

    clip_start_row = (jnp.zeros((SPEAKER_COUNT, ADAPTER_RANK, MODEL_WIDTH), jnp.float32), jnp.zeros((SPEAKER_COUNT, ADAPTER_RANK, VALUE_WIDTH), jnp.float32))
    gradient_totals, adapter_gradient = lax.scan(single_clip_step, clip_start_row, (clip_token_rows, clip_output_gradient, speaker_of_clip))
    down_grad, up_grad = gradient_totals
    adapter_gradient = lax.optimization_barrier(adapter_gradient.reshape(TOKEN_TOTAL, MODEL_WIDTH))
    input_row_gradient = (frozen_gradient + adapter_gradient.astype(jnp.float32)).astype(jnp.bfloat16)
    return input_row_gradient, down_grad, up_grad
```

```python
import functools

import jax
import jax.numpy as jnp
from jax import lax
from jax.experimental import pallas as pl
from jax.experimental.pallas import tpu as pltpu
from jax.sharding import PartitionSpec as P

CAP = 2


def shards(
    tokens, cotangent, frozen_value_weight, adapter_down_weight, adapter_up_weight, speaker_of_clip
):
    owners = lax.axis_size("owner")
    my_index = lax.axis_index("owner")
    core_index = lax.axis_index("tensor")
    clip_count = speaker_of_clip.shape[0] // owners
    clip_rows = tokens.shape[0] // clip_count
    model_width_half = tokens.shape[1]
    value_width_half = adapter_up_weight.shape[2]
    slot_count = owners * CAP
    contract_last = (((1,), (1,)), ((), ()))
    contract_leading = (((0,), (0,)), ((), ()))
    my_clips = lax.dynamic_slice_in_dim(speaker_of_clip, my_index * clip_count, clip_count)
    clip_order = jnp.arange(clip_count)
    earlier = (my_clips[:, None] == my_clips[None, :]) & (clip_order[None, :] < clip_order[:, None])
    position = jnp.sum(earlier.astype(jnp.int32), axis=1)
    target = my_clips * CAP + position
    placing = (jnp.arange(slot_count)[:, None] == target[None, :]).astype(jnp.bfloat16)
    value_rows = lax.dynamic_slice_in_dim(
        cotangent, core_index * value_width_half, value_width_half, 1
    )
    send_tokens = jnp.dot(
        placing, tokens.reshape(clip_count, -1), preferred_element_type=jnp.float32
    )
    send_tokens = send_tokens.astype(jnp.bfloat16).reshape(
        owners, CAP * clip_rows, model_width_half
    )
    send_values = jnp.dot(
        placing, value_rows.reshape(clip_count, -1), preferred_element_type=jnp.float32
    )
    send_values = send_values.astype(jnp.bfloat16).reshape(
        owners, CAP * clip_rows, value_width_half
    )
    got_tokens, got_values = (
        lax.all_to_all(send_tokens, "owner", split_axis=0, concat_axis=0, tiled=True),
        lax.all_to_all(send_values, "owner", split_axis=0, concat_axis=0, tiled=True),
    )
    in_rows = got_tokens.reshape(-1, model_width_half)
    in_values = got_values.reshape(-1, value_width_half)
    down_gradient_local = adapter_down_weight[0]
    up_gradient_local = adapter_up_weight[0]
    acts_part = lax.dot_general(
        down_gradient_local, in_rows, contract_last, preferred_element_type=jnp.float32
    )
    back_part = lax.dot_general(
        up_gradient_local, in_values, contract_last, preferred_element_type=jnp.float32
    )
    acts_sum, back_sum = lax.psum((acts_part, back_part), "tensor")
    acts_low = acts_sum.astype(jnp.bfloat16)
    low_rank_gradient = back_sum.astype(jnp.bfloat16)
    down_grad = jnp.dot(low_rank_gradient, in_rows, preferred_element_type=jnp.float32)[None]
    up_grad = jnp.dot(acts_low, in_values, preferred_element_type=jnp.float32)[None]
    frozen_gradient = lax.dot_general(
        cotangent, frozen_value_weight, contract_last, preferred_element_type=jnp.float32
    )
    slot_terms = lax.dot_general(
        low_rank_gradient, down_gradient_local, contract_leading, preferred_element_type=jnp.float32
    )
    slot_terms = slot_terms.astype(jnp.bfloat16).reshape(owners, CAP * clip_rows, model_width_half)
    returned = lax.all_to_all(slot_terms, "owner", split_axis=0, concat_axis=0, tiled=True)
    adapter_gradient = lax.dot_general(
        placing,
        returned.reshape(slot_count, -1),
        contract_leading,
        preferred_element_type=jnp.float32,
    )
    adapter_gradient = adapter_gradient.reshape(-1, model_width_half)
    input_row_gradient = (frozen_gradient + adapter_gradient).astype(jnp.bfloat16)
    return (input_row_gradient, down_grad, up_grad)


PLANE = 4
MESH = pl.DeviceIdType.MESH
NT = (((1,), (1,)), ((), ()))


def dot(a, b):
    return jnp.dot(a, b, preferred_element_type=jnp.float32)


def slot_starts(clips_ref, first, clip_count, clip_rows, layers, block):
    speakers = [clips_ref[first + j] for j in range(clip_count)]
    starts = []
    for j in range(clip_count):
        position = jnp.int32(0)
        for i in range(j):
            position = position + jnp.where(speakers[i] == speakers[j], 1, 0)
        speaker = speakers[j]
        column = lax.rem(speaker, PLANE)
        layer = lax.div(speaker, PLANE)
        starts.append(column * block + layer * (CAP * clip_rows) + position * clip_rows)
    return starts


def placed_rows(starts, shape, dim, clip_rows):
    token = lax.broadcasted_iota(jnp.int32, shape, dim)
    clip = lax.div(token, clip_rows)
    target = lax.rem(token, clip_rows)
    for j, start in enumerate(starts):
        target = target + jnp.where(clip == j, start, 0)
    return target


def kernel(
    layers,
    clip_count,
    clip_rows,
    chunks,
    clips_ref,
    tokens_ref,
    cotangent_ref,
    down_ref,
    up_ref,
    frozen_ref,
    out_ref,
    down_grad_ref,
    up_grad_ref,
    frozen,
    place,
    unplace,
    send_t,
    send_c,
    got_t,
    got_c,
    all_down,
    all_up,
    low,
    low_t,
    acts,
    terms,
    back,
    send_g,
    got_g,
    send_u,
    got_u,
    base,
    frozen_sem,
    t_sem,
    c_sem,
    d_sem,
    u_sem,
    r_sem,
    g_sem,
    v_sem,
):
    me = lax.axis_index("owner")
    column = me % PLANE
    layer = me // PLANE
    rows = tokens_ref.shape[0]
    width = tokens_ref.shape[1] // chunks
    rank = down_ref.shape[0]
    block = layers * CAP * clip_rows
    slots = PLANE * block
    all_rank = layers * rank

    frozen_copy = pltpu.make_async_copy(frozen_ref, frozen, frozen_sem)
    frozen_copy.start()

    def in_plane(j):
        return layer * PLANE + (column + j) % PLANE

    def in_line(j):
        return ((layer + j) % layers) * PLANE + column

    barrier = pltpu.get_barrier_semaphore()
    for j in range(1, PLANE):
        pl.semaphore_signal(barrier, inc=1, device_id={"owner": in_plane(j)}, device_id_type=MESH)
    for j in range(1, layers):
        pl.semaphore_signal(barrier, inc=1, device_id={"owner": in_line(j)}, device_id_type=MESH)
    pl.semaphore_wait(barrier, PLANE - 1 + layers - 1)

    def remote(src, dst, sems, at, owner):
        return pltpu.make_async_remote_copy(
            src_ref=src,
            dst_ref=dst,
            send_sem=sems.at[(0,) + at],
            recv_sem=sems.at[(1,) + at],
            device_id={"owner": owner},
            device_id_type=MESH,
        )

    def span(k):
        return pl.ds(pl.multiple_of(k * width, width), width)

    def up_copy(j):
        return remote(up_ref, all_up.at[layer], u_sem, (j,), in_line(j))

    def down_copy(k, j):
        return remote(
            down_ref.at[:, span(k)], all_down.at[k, layer], d_sem, (k, j), in_line(j)
        )

    def value_copy(j):
        return remote(
            send_c.at[(column + j) % PLANE], got_c.at[column], c_sem, (j,), in_plane(j)
        )

    def token_copy(k, j):
        return remote(
            send_t.at[k, (column + j) % PLANE], got_t.at[k, column], t_sem, (k, j), in_plane(j)
        )

    def term_copy(k, j):
        return remote(
            terms.at[k, (column + j) % PLANE], back.at[k, column], r_sem, (k, j), in_plane(j)
        )

    def grad_copy(k, j):
        return remote(
            send_g.at[k, (layer + j) % layers], got_g.at[k, j], g_sem, (k, j), in_line(j)
        )

    def up_grad_copy(j):
        return remote(send_u.at[(layer + j) % layers], got_u.at[j], v_sem, (j,), in_line(j))

    for j in range(1, layers):
        up_copy(j).start()

    starts = slot_starts(clips_ref, me * clip_count, clip_count, clip_rows, layers, block)
    slot = lax.broadcasted_iota(jnp.int32, (slots, rows), 0)
    target = placed_rows(starts, (slots, rows), 1, clip_rows)
    place[...] = jnp.where(slot == target, 1.0, 0.0).astype(jnp.bfloat16)
    slot = lax.broadcasted_iota(jnp.int32, (rows, slots), 1)
    target = placed_rows(starts, (rows, slots), 0, clip_rows)
    unplace[...] = jnp.where(slot == target, 1.0, 0.0).astype(jnp.bfloat16)

    send_c[...] = (
        dot(place[...], cotangent_ref[...]).astype(jnp.bfloat16).reshape(send_c.shape)
    )
    for j in range(1, PLANE):
        value_copy(j).start()

    @pl.loop(0, chunks)
    def _(k):
        for j in range(1, layers):
            down_copy(k, j).start()
        placed = dot(place[...], tokens_ref[:, span(k)]).astype(jnp.bfloat16)
        send_t[k] = placed.reshape(PLANE, block, width)
        for j in range(1, PLANE):
            token_copy(k, j).start()
        got_t[k, column] = send_t[k, column]
        all_down[k, layer] = down_ref[:, span(k)]

    got_c[column] = send_c[column]
    all_up[layer] = up_ref[...]
    frozen_copy.wait()

    @pl.loop(0, chunks)
    def _(k):
        base[k] = lax.dot_general(
            cotangent_ref[...],
            frozen[span(k), :],
            NT,
            preferred_element_type=jnp.float32,
        )

    for j in range(1, layers):
        up_copy(j).wait_recv()
    for j in range(1, PLANE):
        value_copy(j).wait_recv()

    def own(shape, slot_dim, rank_dim):
        slot_layer = lax.div(
            lax.rem(lax.broadcasted_iota(jnp.int32, shape, slot_dim), block), CAP * clip_rows
        )
        return slot_layer == lax.div(lax.broadcasted_iota(jnp.int32, shape, rank_dim), rank)

    values = got_c[...].reshape(slots, got_c.shape[2])
    ups = all_up[...].reshape(all_rank, all_up.shape[2])
    full = lax.dot_general(values, ups, NT, preferred_element_type=jnp.float32)
    low[...] = jnp.where(own((slots, all_rank), 0, 1), full, 0.0).astype(jnp.bfloat16)
    full = lax.dot_general(ups, values, NT, preferred_element_type=jnp.float32)
    low_t[...] = jnp.where(own((all_rank, slots), 1, 0), full, 0.0).astype(jnp.bfloat16)
    acts[...] = jnp.zeros_like(acts)

    @pl.loop(0, chunks)
    def _(k):
        for j in range(1, layers):
            down_copy(k, j).wait_recv()
        downs = all_down[k].reshape(all_rank, width)
        term = dot(low[...], downs).astype(jnp.bfloat16).reshape(PLANE, block, width)
        terms[k] = term
        for j in range(1, PLANE):
            term_copy(k, j).start()
        back[k, column] = terms[k, column]
        for j in range(1, PLANE):
            token_copy(k, j).wait_recv()
        tokens = got_t[k].reshape(slots, width)
        grad = dot(low_t[...], tokens).reshape(layers, rank, width)
        send_g[k] = grad.astype(jnp.bfloat16)
        for j in range(1, layers):
            grad_copy(k, j).start()
        down_grad_ref[:, span(k)] = lax.dot_general(
            low_t[pl.ds(pl.multiple_of(layer * rank, rank), rank), :],
            tokens,
            (((1,), (0,)), ((), ())),
            preferred_element_type=jnp.float32,
        )
        acts[...] += lax.dot_general(downs, tokens, NT, preferred_element_type=jnp.float32)

    acts_low = jnp.where(own((all_rank, slots), 1, 0), acts[...], 0.0).astype(jnp.bfloat16)
    grad = dot(acts_low, got_c[...].reshape(slots, got_c.shape[2]))
    base_u = grad.reshape(layers, rank, got_c.shape[2])
    send_u[...] = base_u.astype(jnp.bfloat16)
    for j in range(1, layers):
        up_grad_copy(j).start()
    mine = jnp.zeros((rank, got_c.shape[2]), jnp.float32)
    for i in range(layers):
        mine = jnp.where(layer == i, base_u[i], mine)
    up_grad_ref[...] = mine

    @pl.loop(0, chunks)
    def _(k):
        for j in range(1, PLANE):
            term_copy(k, j).wait_recv()
        returned = dot(unplace[...], back[k].reshape(slots, width))
        out_ref[:, span(k)] = (base[k] + returned).astype(jnp.bfloat16)

    @pl.loop(0, chunks)
    def _(k):
        total = down_grad_ref[:, span(k)]
        for j in range(1, layers):
            grad_copy(k, j).wait_recv()
            total = total + got_g[k, j].astype(jnp.float32)
        down_grad_ref[:, span(k)] = total

    total = up_grad_ref[...]
    for j in range(1, layers):
        up_grad_copy(j).wait_recv()
        total = total + got_u[j].astype(jnp.float32)
    up_grad_ref[...] = total

    for j in range(1, layers):
        up_copy(j).wait_send()
        up_grad_copy(j).wait_send()
    for j in range(1, PLANE):
        value_copy(j).wait_send()

    @pl.loop(0, chunks)
    def _(k):
        for j in range(1, layers):
            down_copy(k, j).wait_send()
            grad_copy(k, j).wait_send()
        for j in range(1, PLANE):
            token_copy(k, j).wait_send()
            term_copy(k, j).wait_send()


def fused(
    tokens, cotangent, frozen_value_weight, adapter_down_weight, adapter_up_weight, speaker_of_clip
):
    owners = lax.axis_size("owner")
    layers = owners // PLANE
    clip_count = speaker_of_clip.shape[0] // owners
    rows, model_width = tokens.shape
    value_width = cotangent.shape[1]
    clip_rows = rows // clip_count
    rank = adapter_down_weight.shape[1]
    chunks = 8
    width = model_width // chunks
    block = layers * CAP * clip_rows
    slots = PLANE * block
    half = jnp.bfloat16
    vmem = pl.BlockSpec(memory_space=pltpu.VMEM)
    dma = pltpu.SemaphoreType.DMA
    out, down_grad, up_grad = pl.pallas_call(
        functools.partial(kernel, layers, clip_count, clip_rows, chunks),
        out_shape=(
            jax.ShapeDtypeStruct((rows, model_width), half),
            jax.ShapeDtypeStruct((rank, model_width), jnp.float32),
            jax.ShapeDtypeStruct((rank, value_width), jnp.float32),
        ),
        in_specs=[pl.BlockSpec(memory_space=pltpu.SMEM)]
        + [vmem] * 4
        + [pl.BlockSpec(memory_space=pl.ANY)],
        out_specs=(vmem, vmem, vmem),
        scratch_shapes=[
            pltpu.VMEM((model_width, value_width), half),
            pltpu.VMEM((slots, rows), half),
            pltpu.VMEM((rows, slots), half),
            pltpu.VMEM((chunks, PLANE, block, width), half),
            pltpu.VMEM((PLANE, block, value_width), half),
            pltpu.VMEM((chunks, PLANE, block, width), half),
            pltpu.VMEM((PLANE, block, value_width), half),
            pltpu.VMEM((chunks, layers, rank, width), half),
            pltpu.VMEM((layers, rank, value_width), half),
            pltpu.VMEM((slots, layers * rank), half),
            pltpu.VMEM((layers * rank, slots), half),
            pltpu.VMEM((layers * rank, slots), jnp.float32),
            pltpu.VMEM((chunks, PLANE, block, width), half),
            pltpu.VMEM((chunks, PLANE, block, width), half),
            pltpu.VMEM((chunks, layers, rank, width), half),
            pltpu.VMEM((chunks, layers, rank, width), half),
            pltpu.VMEM((layers, rank, value_width), half),
            pltpu.VMEM((layers, rank, value_width), half),
            pltpu.VMEM((chunks, rows, width), jnp.float32),
            dma(()),
            dma((2, chunks, PLANE)),
            dma((2, PLANE)),
            dma((2, chunks, layers)),
            dma((2, layers)),
            dma((2, chunks, PLANE)),
            dma((2, chunks, layers)),
            dma((2, layers)),
        ],
        compiler_params=pltpu.CompilerParams(
            collective_id=0, has_side_effects=True, vmem_limit_bytes=56 * 2**20
        ),
        cost_estimate=pl.CostEstimate(
            flops=8 * 10**9, bytes_accessed=16 * 2**20, transcendentals=0
        ),
    )(
        speaker_of_clip,
        tokens,
        cotangent,
        adapter_down_weight[0],
        adapter_up_weight[0],
        frozen_value_weight,
    )
    return out, down_grad[None], up_grad[None]


def solution(mesh):
    body = fused if mesh.shape["tensor"] == 1 and mesh.shape["owner"] == 16 else shards
    return jax.shard_map(
        body,
        mesh=mesh,
        in_specs=(
            P(("groups", "owner"), "tensor"),
            P(("groups", "owner"), None),
            P("tensor", None),
            P("owner", None, "tensor"),
            P("owner", None, "tensor"),
            P("groups"),
        ),
        out_specs=(
            P(("groups", "owner"), "tensor"),
            P(("groups", "owner"), None, "tensor"),
            P(("groups", "owner"), None, "tensor"),
        ),
        check_vma=False,
    )
```

```python
import functools

import jax
import jax.numpy as jnp
from jax import lax
from jax.experimental import pallas as pl
from jax.experimental.pallas import tpu as pltpu
from jax.sharding import PartitionSpec as P

CAP = 2


def shards(
    tokens, cotangent, frozen_value_weight, adapter_down_weight, adapter_up_weight, speaker_of_clip
):
    owners = lax.axis_size("owner")
    my_index = lax.axis_index("owner")
    core_index = lax.axis_index("tensor")
    clip_count = speaker_of_clip.shape[0] // owners
    clip_rows = tokens.shape[0] // clip_count
    model_width_half = tokens.shape[1]
    value_width_half = adapter_up_weight.shape[2]
    slot_count = owners * CAP
    contract_last = (((1,), (1,)), ((), ()))
    contract_leading = (((0,), (0,)), ((), ()))
    my_clips = lax.dynamic_slice_in_dim(speaker_of_clip, my_index * clip_count, clip_count)
    clip_order = jnp.arange(clip_count)
    earlier = (my_clips[:, None] == my_clips[None, :]) & (clip_order[None, :] < clip_order[:, None])
    position = jnp.sum(earlier.astype(jnp.int32), axis=1)
    target = my_clips * CAP + position
    placing = (jnp.arange(slot_count)[:, None] == target[None, :]).astype(jnp.bfloat16)
    value_rows = lax.dynamic_slice_in_dim(
        cotangent, core_index * value_width_half, value_width_half, 1
    )
    send_tokens = jnp.dot(
        placing, tokens.reshape(clip_count, -1), preferred_element_type=jnp.float32
    )
    send_tokens = send_tokens.astype(jnp.bfloat16).reshape(
        owners, CAP * clip_rows, model_width_half
    )
    send_values = jnp.dot(
        placing, value_rows.reshape(clip_count, -1), preferred_element_type=jnp.float32
    )
    send_values = send_values.astype(jnp.bfloat16).reshape(
        owners, CAP * clip_rows, value_width_half
    )
    got_tokens, got_values = (
        lax.all_to_all(send_tokens, "owner", split_axis=0, concat_axis=0, tiled=True),
        lax.all_to_all(send_values, "owner", split_axis=0, concat_axis=0, tiled=True),
    )
    in_rows = got_tokens.reshape(-1, model_width_half)
    in_values = got_values.reshape(-1, value_width_half)
    down_gradient_local = adapter_down_weight[0]
    up_gradient_local = adapter_up_weight[0]
    acts_part = lax.dot_general(
        down_gradient_local, in_rows, contract_last, preferred_element_type=jnp.float32
    )
    back_part = lax.dot_general(
        up_gradient_local, in_values, contract_last, preferred_element_type=jnp.float32
    )
    acts_sum, back_sum = lax.psum((acts_part, back_part), "tensor")
    acts_low = acts_sum.astype(jnp.bfloat16)
    low_rank_gradient = back_sum.astype(jnp.bfloat16)
    down_grad = jnp.dot(low_rank_gradient, in_rows, preferred_element_type=jnp.float32)[None]
    up_grad = jnp.dot(acts_low, in_values, preferred_element_type=jnp.float32)[None]
    frozen_gradient = lax.dot_general(
        cotangent, frozen_value_weight, contract_last, preferred_element_type=jnp.float32
    )
    slot_terms = lax.dot_general(
        low_rank_gradient, down_gradient_local, contract_leading, preferred_element_type=jnp.float32
    )
    slot_terms = slot_terms.astype(jnp.bfloat16).reshape(owners, CAP * clip_rows, model_width_half)
    returned = lax.all_to_all(slot_terms, "owner", split_axis=0, concat_axis=0, tiled=True)
    adapter_gradient = lax.dot_general(
        placing,
        returned.reshape(slot_count, -1),
        contract_leading,
        preferred_element_type=jnp.float32,
    )
    adapter_gradient = adapter_gradient.reshape(-1, model_width_half)
    input_row_gradient = (frozen_gradient + adapter_gradient).astype(jnp.bfloat16)
    return (input_row_gradient, down_grad, up_grad)


PLANE = 4
AHEAD = 2
LAG = 2
MESH = pl.DeviceIdType.MESH
NT = (((1,), (1,)), ((), ()))


def dot(a, b):
    return jnp.dot(a, b, preferred_element_type=jnp.float32)


def slot_starts(clips_ref, first, clip_count, clip_rows, layers, block):
    speakers = [clips_ref[first + j] for j in range(clip_count)]
    starts = []
    for j in range(clip_count):
        position = jnp.int32(0)
        for i in range(j):
            position = position + jnp.where(speakers[i] == speakers[j], 1, 0)
        speaker = speakers[j]
        column = lax.rem(speaker, PLANE)
        layer = lax.div(speaker, PLANE)
        starts.append(column * block + layer * (CAP * clip_rows) + position * clip_rows)
    return starts


def placed_rows(starts, shape, dim, clip_rows):
    token = lax.broadcasted_iota(jnp.int32, shape, dim)
    clip = lax.div(token, clip_rows)
    target = lax.rem(token, clip_rows)
    for j, start in enumerate(starts):
        target = target + jnp.where(clip == j, start, 0)
    return target


def kernel(
    layers,
    clip_count,
    clip_rows,
    chunks,
    clips_ref,
    tokens_ref,
    cotangent_ref,
    down_ref,
    up_ref,
    frozen_ref,
    out_ref,
    down_grad_ref,
    up_grad_ref,
    frozen,
    place,
    unplace,
    send_t,
    send_c,
    got_t,
    got_c,
    all_down,
    all_up,
    low,
    low_t,
    acts,
    terms,
    back,
    grad,
    keep,
    send_g,
    got_g,
    far_g,
    in_g,
    keep_u,
    send_u,
    got_u,
    far_u,
    in_u,
    base,
    frozen_sem,
    t_sem,
    c_sem,
    d_sem,
    u_sem,
    r_sem,
    g_sem,
    h_sem,
    v_sem,
    w_sem,
    x_sem,
    y_sem,
):
    me = lax.axis_index("owner")
    group = lax.axis_index("groups")
    column = me % PLANE
    layer = me // PLANE
    carrier = column % 2 == group
    pair = layer + 1 - 2 * (layer % 2)
    far = (layer + 2) % layers
    pair_far = (pair + 2) % layers
    rows = tokens_ref.shape[0]
    width = tokens_ref.shape[1] // chunks
    rank = down_ref.shape[0]
    block = layers * CAP * clip_rows
    slots = PLANE * block
    all_rank = layers * rank

    frozen_copy = pltpu.make_async_copy(frozen_ref, frozen, frozen_sem)
    frozen_copy.start()

    def in_plane(j):
        return layer * PLANE + (column + j) % PLANE

    def in_line(j):
        return ((layer + j) % layers) * PLANE + column

    barrier = pltpu.get_barrier_semaphore()
    for j in range(1, PLANE):
        pl.semaphore_signal(barrier, inc=1, device_id={"owner": in_plane(j)}, device_id_type=MESH)
    for j in range(1, layers):
        pl.semaphore_signal(barrier, inc=1, device_id={"owner": in_line(j)}, device_id_type=MESH)
    across = {"groups": 1 - group, "owner": me}
    pl.semaphore_signal(barrier, inc=1, device_id=across, device_id_type=MESH)
    pl.semaphore_wait(barrier, PLANE - 1 + layers - 1 + 1)

    def remote(src, dst, sems, at, owner):
        return pltpu.make_async_remote_copy(
            src_ref=src,
            dst_ref=dst,
            send_sem=sems.at[(0,) + at],
            recv_sem=sems.at[(1,) + at],
            device_id={"owner": owner},
            device_id_type=MESH,
        )

    def span(k):
        return pl.ds(pl.multiple_of(k * width, width), width)

    def up_copy(j):
        return remote(up_ref, all_up.at[layer], u_sem, (j,), in_line(j))

    def down_copy(k, j):
        return remote(
            down_ref.at[:, span(k)], all_down.at[k, layer], d_sem, (k, j), in_line(j)
        )

    def value_copy(j):
        return remote(
            send_c.at[(column + j) % PLANE], got_c.at[column], c_sem, (j,), in_plane(j)
        )

    def token_copy(k, j):
        return remote(
            send_t.at[k, (column + j) % PLANE], got_t.at[k, column], t_sem, (k, j), in_plane(j)
        )

    def term_copy(k, j):
        return remote(
            terms.at[k, (column + j) % PLANE], back.at[k, column], r_sem, (k, j), in_plane(j)
        )

    def grad_copy(k):
        return remote(send_g.at[k], got_g.at[k], g_sem, (k,), pair * PLANE + column)

    def far_copy(k):
        return remote(far_g.at[k], in_g.at[k], h_sem, (k,), far * PLANE + column)

    def up_grad_copy():
        return remote(send_u, got_u, v_sem, (0,), pair * PLANE + column)

    def up_far_copy():
        return remote(far_u, in_u, w_sem, (0,), far * PLANE + column)

    def hand(ref, sems, at):
        return pltpu.make_async_remote_copy(
            src_ref=ref,
            dst_ref=ref,
            send_sem=sems.at[(0,) + at],
            recv_sem=sems.at[(1,) + at],
            device_id=across,
            device_id_type=MESH,
        )

    def hand_down(k, j):
        return hand(all_down.at[k, (layer - j + layers) % layers], x_sem, (k, j))

    def hand_up(j):
        return hand(all_up.at[(layer - j + layers) % layers], y_sem, (j,))

    def pass_down(k):
        @pl.when(carrier)
        def _():
            for j in range(1, layers):
                down_copy(k, j).wait_recv()
                hand_down(k, j).start()

    @pl.when(carrier)
    def _():
        for j in range(1, layers):
            up_copy(j).start()

    starts = slot_starts(clips_ref, me * clip_count, clip_count, clip_rows, layers, block)
    slot = lax.broadcasted_iota(jnp.int32, (slots, rows), 0)
    target = placed_rows(starts, (slots, rows), 1, clip_rows)
    place[...] = jnp.where(slot == target, 1.0, 0.0).astype(jnp.bfloat16)
    slot = lax.broadcasted_iota(jnp.int32, (rows, slots), 1)
    target = placed_rows(starts, (rows, slots), 0, clip_rows)
    unplace[...] = jnp.where(slot == target, 1.0, 0.0).astype(jnp.bfloat16)

    send_c[...] = (
        dot(place[...], cotangent_ref[...]).astype(jnp.bfloat16).reshape(send_c.shape)
    )
    for j in range(1, PLANE):
        value_copy(j).start()

    @pl.loop(0, chunks)
    def _(k):
        @pl.when(carrier)
        def _():
            for j in range(1, layers):
                down_copy(k, j).start()

        placed = dot(place[...], tokens_ref[:, span(k)]).astype(jnp.bfloat16)
        send_t[k] = placed.reshape(PLANE, block, width)
        for j in range(1, PLANE):
            token_copy(k, j).start()
        got_t[k, column] = send_t[k, column]
        all_down[k, layer] = down_ref[:, span(k)]

    got_c[column] = send_c[column]
    all_up[layer] = up_ref[...]
    frozen_copy.wait()

    @pl.loop(0, chunks)
    def _(k):
        base[k] = lax.dot_general(
            cotangent_ref[...],
            frozen[span(k), :],
            NT,
            preferred_element_type=jnp.float32,
        )

    @pl.when(carrier)
    def _():
        for j in range(1, layers):
            up_copy(j).wait_recv()
            hand_up(j).start()

    for k in range(AHEAD):
        pass_down(k)

    @pl.when(jnp.logical_not(carrier))
    def _():
        for j in range(1, layers):
            hand_up(j).wait_recv()

    for j in range(1, PLANE):
        value_copy(j).wait_recv()

    def own(shape, slot_dim, rank_dim):
        slot_layer = lax.div(
            lax.rem(lax.broadcasted_iota(jnp.int32, shape, slot_dim), block), CAP * clip_rows
        )
        return slot_layer == lax.div(lax.broadcasted_iota(jnp.int32, shape, rank_dim), rank)

    values = got_c[...].reshape(slots, got_c.shape[2])
    ups = all_up[...].reshape(all_rank, all_up.shape[2])
    full = lax.dot_general(values, ups, NT, preferred_element_type=jnp.float32)
    low[...] = jnp.where(own((slots, all_rank), 0, 1), full, 0.0).astype(jnp.bfloat16)
    full = lax.dot_general(ups, values, NT, preferred_element_type=jnp.float32)
    low_t[...] = jnp.where(own((all_rank, slots), 1, 0), full, 0.0).astype(jnp.bfloat16)
    acts[...] = jnp.zeros_like(acts)

    def pass_grad(k):
        grad_copy(k).wait_recv()
        far_g[k] = (keep[k] + got_g[k, 1].astype(jnp.float32)).astype(jnp.bfloat16)
        far_copy(k).start()

    @pl.loop(0, chunks)
    def _(k):
        @pl.when(k + AHEAD < chunks)
        def _():
            pass_down(k + AHEAD)

        @pl.when(jnp.logical_not(carrier))
        def _():
            for j in range(1, layers):
                hand_down(k, j).wait_recv()

        downs = all_down[k].reshape(all_rank, width)
        term = dot(low[...], downs).astype(jnp.bfloat16).reshape(PLANE, block, width)
        terms[k] = term
        for j in range(1, PLANE):
            term_copy(k, j).start()
        back[k, column] = terms[k, column]
        for j in range(1, PLANE):
            token_copy(k, j).wait_recv()
        tokens = got_t[k].reshape(slots, width)
        grad[...] = dot(low_t[...], tokens).reshape(layers, rank, width)
        send_g[k, 0] = grad[pair].astype(jnp.bfloat16)
        send_g[k, 1] = grad[pair_far].astype(jnp.bfloat16)
        grad_copy(k).start()
        down_grad_ref[:, span(k)] = grad[layer]
        keep[k] = grad[far]
        acts[...] += lax.dot_general(downs, tokens, NT, preferred_element_type=jnp.float32)

        @pl.when(k >= LAG)
        def _():
            pass_grad(k - LAG)

    acts_low = jnp.where(own((all_rank, slots), 1, 0), acts[...], 0.0).astype(jnp.bfloat16)
    keep_u[...] = dot(acts_low, got_c[...].reshape(slots, got_c.shape[2])).reshape(keep_u.shape)
    send_u[0] = keep_u[pair].astype(jnp.bfloat16)
    send_u[1] = keep_u[pair_far].astype(jnp.bfloat16)
    up_grad_copy().start()

    for k in range(chunks - LAG, chunks):
        pass_grad(k)
    up_grad_copy().wait_recv()
    far_u[...] = (keep_u[far] + got_u[1].astype(jnp.float32)).astype(jnp.bfloat16)
    up_far_copy().start()

    @pl.loop(0, chunks)
    def _(k):
        for j in range(1, PLANE):
            term_copy(k, j).wait_recv()
        returned = dot(unplace[...], back[k].reshape(slots, width))
        out_ref[:, span(k)] = (base[k] + returned).astype(jnp.bfloat16)

    @pl.loop(0, chunks)
    def _(k):
        far_copy(k).wait_recv()
        down_grad_ref[:, span(k)] = (
            down_grad_ref[:, span(k)]
            + got_g[k, 0].astype(jnp.float32)
            + in_g[k].astype(jnp.float32)
        )

    up_far_copy().wait_recv()
    up_grad_ref[...] = (
        keep_u[layer] + got_u[0].astype(jnp.float32) + in_u[...].astype(jnp.float32)
    )

    up_grad_copy().wait_send()
    up_far_copy().wait_send()
    for j in range(1, PLANE):
        value_copy(j).wait_send()

    @pl.when(carrier)
    def _():
        for j in range(1, layers):
            up_copy(j).wait_send()
            hand_up(j).wait_send()

    @pl.loop(0, chunks)
    def _(k):
        grad_copy(k).wait_send()
        far_copy(k).wait_send()
        for j in range(1, PLANE):
            token_copy(k, j).wait_send()
            term_copy(k, j).wait_send()

        @pl.when(carrier)
        def _():
            for j in range(1, layers):
                down_copy(k, j).wait_send()
                hand_down(k, j).wait_send()


def fused(
    tokens, cotangent, frozen_value_weight, adapter_down_weight, adapter_up_weight, speaker_of_clip
):
    owners = lax.axis_size("owner")
    layers = owners // PLANE
    clip_count = speaker_of_clip.shape[0] // owners
    rows, model_width = tokens.shape
    value_width = cotangent.shape[1]
    clip_rows = rows // clip_count
    rank = adapter_down_weight.shape[1]
    chunks = 8
    width = model_width // chunks
    block = layers * CAP * clip_rows
    slots = PLANE * block
    half = jnp.bfloat16
    vmem = pl.BlockSpec(memory_space=pltpu.VMEM)
    dma = pltpu.SemaphoreType.DMA
    out, down_grad, up_grad = pl.pallas_call(
        functools.partial(kernel, layers, clip_count, clip_rows, chunks),
        out_shape=(
            jax.ShapeDtypeStruct((rows, model_width), half),
            jax.ShapeDtypeStruct((rank, model_width), jnp.float32),
            jax.ShapeDtypeStruct((rank, value_width), jnp.float32),
        ),
        in_specs=[pl.BlockSpec(memory_space=pltpu.SMEM)]
        + [vmem] * 4
        + [pl.BlockSpec(memory_space=pl.ANY)],
        out_specs=(vmem, vmem, vmem),
        scratch_shapes=[
            pltpu.VMEM((model_width, value_width), half),
            pltpu.VMEM((slots, rows), half),
            pltpu.VMEM((rows, slots), half),
            pltpu.VMEM((chunks, PLANE, block, width), half),
            pltpu.VMEM((PLANE, block, value_width), half),
            pltpu.VMEM((chunks, PLANE, block, width), half),
            pltpu.VMEM((PLANE, block, value_width), half),
            pltpu.VMEM((chunks, layers, rank, width), half),
            pltpu.VMEM((layers, rank, value_width), half),
            pltpu.VMEM((slots, layers * rank), half),
            pltpu.VMEM((layers * rank, slots), half),
            pltpu.VMEM((layers * rank, slots), jnp.float32),
            pltpu.VMEM((chunks, PLANE, block, width), half),
            pltpu.VMEM((chunks, PLANE, block, width), half),
            pltpu.VMEM((layers, rank, width), jnp.float32),
            pltpu.VMEM((chunks, rank, width), jnp.float32),
            pltpu.VMEM((chunks, 2, rank, width), half),
            pltpu.VMEM((chunks, 2, rank, width), half),
            pltpu.VMEM((chunks, rank, width), half),
            pltpu.VMEM((chunks, rank, width), half),
            pltpu.VMEM((layers, rank, value_width), jnp.float32),
            pltpu.VMEM((2, rank, value_width), half),
            pltpu.VMEM((2, rank, value_width), half),
            pltpu.VMEM((rank, value_width), half),
            pltpu.VMEM((rank, value_width), half),
            pltpu.VMEM((chunks, rows, width), jnp.float32),
            dma(()),
            dma((2, chunks, PLANE)),
            dma((2, PLANE)),
            dma((2, chunks, layers)),
            dma((2, layers)),
            dma((2, chunks, PLANE)),
            dma((2, chunks)),
            dma((2, chunks)),
            dma((2, 1)),
            dma((2, 1)),
            dma((2, chunks, layers)),
            dma((2, layers)),
        ],
        compiler_params=pltpu.CompilerParams(
            collective_id=0, has_side_effects=True, vmem_limit_bytes=56 * 2**20
        ),
        cost_estimate=pl.CostEstimate(
            flops=8 * 10**9, bytes_accessed=16 * 2**20, transcendentals=0
        ),
    )(
        speaker_of_clip,
        tokens,
        cotangent,
        adapter_down_weight[0],
        adapter_up_weight[0],
        frozen_value_weight,
    )
    return out, down_grad[None], up_grad[None]


def solution(mesh):
    sizes = [mesh.shape[axis] for axis in ("groups", "owner", "tensor")]
    body = fused if sizes == [2, 16, 1] else shards
    return jax.shard_map(
        body,
        mesh=mesh,
        in_specs=(
            P(("groups", "owner"), "tensor"),
            P(("groups", "owner"), None),
            P("tensor", None),
            P("owner", None, "tensor"),
            P("owner", None, "tensor"),
            P("groups"),
        ),
        out_specs=(
            P(("groups", "owner"), "tensor"),
            P(("groups", "owner"), None, "tensor"),
            P(("groups", "owner"), None, "tensor"),
        ),
        check_vma=False,
    )
```

```python
import functools

import jax
import jax.numpy as jnp
from jax import lax
from jax.experimental import pallas as pl
from jax.experimental.pallas import tpu as pltpu
from jax.sharding import PartitionSpec as P

CAP = 2


def shards(
    tokens, cotangent, frozen_value_weight, adapter_down_weight, adapter_up_weight, speaker_of_clip
):
    owners = lax.axis_size("owner")
    my_index = lax.axis_index("owner")
    core_index = lax.axis_index("tensor")
    clip_count = speaker_of_clip.shape[0] // owners
    clip_rows = tokens.shape[0] // clip_count
    model_width_half = tokens.shape[1]
    value_width_half = adapter_up_weight.shape[2]
    slot_count = owners * CAP
    contract_last = (((1,), (1,)), ((), ()))
    contract_leading = (((0,), (0,)), ((), ()))
    my_clips = lax.dynamic_slice_in_dim(speaker_of_clip, my_index * clip_count, clip_count)
    clip_order = jnp.arange(clip_count)
    earlier = (my_clips[:, None] == my_clips[None, :]) & (clip_order[None, :] < clip_order[:, None])
    position = jnp.sum(earlier.astype(jnp.int32), axis=1)
    target = my_clips * CAP + position
    placing = (jnp.arange(slot_count)[:, None] == target[None, :]).astype(jnp.bfloat16)
    value_rows = lax.dynamic_slice_in_dim(
        cotangent, core_index * value_width_half, value_width_half, 1
    )
    send_tokens = jnp.dot(
        placing, tokens.reshape(clip_count, -1), preferred_element_type=jnp.float32
    )
    send_tokens = send_tokens.astype(jnp.bfloat16).reshape(
        owners, CAP * clip_rows, model_width_half
    )
    send_values = jnp.dot(
        placing, value_rows.reshape(clip_count, -1), preferred_element_type=jnp.float32
    )
    send_values = send_values.astype(jnp.bfloat16).reshape(
        owners, CAP * clip_rows, value_width_half
    )
    got_tokens, got_values = (
        lax.all_to_all(send_tokens, "owner", split_axis=0, concat_axis=0, tiled=True),
        lax.all_to_all(send_values, "owner", split_axis=0, concat_axis=0, tiled=True),
    )
    in_rows = got_tokens.reshape(-1, model_width_half)
    in_values = got_values.reshape(-1, value_width_half)
    down_gradient_local = adapter_down_weight[0]
    up_gradient_local = adapter_up_weight[0]
    acts_part = lax.dot_general(
        down_gradient_local, in_rows, contract_last, preferred_element_type=jnp.float32
    )
    back_part = lax.dot_general(
        up_gradient_local, in_values, contract_last, preferred_element_type=jnp.float32
    )
    acts_sum, back_sum = lax.psum((acts_part, back_part), "tensor")
    acts_low = acts_sum.astype(jnp.bfloat16)
    low_rank_gradient = back_sum.astype(jnp.bfloat16)
    down_grad = jnp.dot(low_rank_gradient, in_rows, preferred_element_type=jnp.float32)[None]
    up_grad = jnp.dot(acts_low, in_values, preferred_element_type=jnp.float32)[None]
    frozen_gradient = lax.dot_general(
        cotangent, frozen_value_weight, contract_last, preferred_element_type=jnp.float32
    )
    slot_terms = lax.dot_general(
        low_rank_gradient, down_gradient_local, contract_leading, preferred_element_type=jnp.float32
    )
    slot_terms = slot_terms.astype(jnp.bfloat16).reshape(owners, CAP * clip_rows, model_width_half)
    returned = lax.all_to_all(slot_terms, "owner", split_axis=0, concat_axis=0, tiled=True)
    adapter_gradient = lax.dot_general(
        placing,
        returned.reshape(slot_count, -1),
        contract_leading,
        preferred_element_type=jnp.float32,
    )
    adapter_gradient = adapter_gradient.reshape(-1, model_width_half)
    input_row_gradient = (frozen_gradient + adapter_gradient).astype(jnp.bfloat16)
    return (input_row_gradient, down_grad, up_grad)


PLANE = 4
AHEAD = 2
LAG = 2
HOLD = 5
MESH = pl.DeviceIdType.MESH
NT = (((1,), (1,)), ((), ()))


def dot(a, b):
    return jnp.dot(a, b, preferred_element_type=jnp.float32)


def slot_starts(clips_ref, first, clip_count, clip_rows, layers, block):
    speakers = [clips_ref[first + j] for j in range(clip_count)]
    starts = []
    for j in range(clip_count):
        position = jnp.int32(0)
        for i in range(j):
            position = position + jnp.where(speakers[i] == speakers[j], 1, 0)
        speaker = speakers[j]
        column = lax.rem(speaker, PLANE)
        layer = lax.div(speaker, PLANE)
        starts.append(column * block + layer * (CAP * clip_rows) + position * clip_rows)
    return starts


def placed_rows(starts, shape, dim, clip_rows):
    token = lax.broadcasted_iota(jnp.int32, shape, dim)
    clip = lax.div(token, clip_rows)
    target = lax.rem(token, clip_rows)
    for j, start in enumerate(starts):
        target = target + jnp.where(clip == j, start, 0)
    return target


def kernel(
    layers,
    clip_count,
    clip_rows,
    chunks,
    clips_ref,
    tokens_ref,
    cotangent_ref,
    down_ref,
    up_ref,
    frozen_ref,
    out_ref,
    down_grad_ref,
    up_grad_ref,
    frozen,
    place,
    unplace,
    send_t,
    send_c,
    got_t,
    got_c,
    all_down,
    all_up,
    low,
    low_t,
    acts,
    terms,
    back,
    grad,
    keep,
    send_g,
    got_g,
    far_g,
    in_g,
    keep_u,
    send_u,
    got_u,
    far_u,
    in_u,
    base,
    frozen_sem,
    t_sem,
    c_sem,
    d_sem,
    u_sem,
    r_sem,
    g_sem,
    h_sem,
    v_sem,
    w_sem,
    x_sem,
    y_sem,
):
    me = lax.axis_index("owner")
    group = lax.axis_index("groups")
    column = me % PLANE
    layer = me // PLANE
    carrier = column % 2 == group
    pair = layer + 1 - 2 * (layer % 2)
    far = (layer + 2) % layers
    pair_far = (pair + 2) % layers
    rows = tokens_ref.shape[0]
    width = tokens_ref.shape[1] // chunks
    rank = down_ref.shape[0]
    block = layers * CAP * clip_rows
    slots = PLANE * block
    all_rank = layers * rank

    frozen_copy = pltpu.make_async_copy(frozen_ref, frozen, frozen_sem)
    frozen_copy.start()

    def in_plane(j):
        return layer * PLANE + (column + j) % PLANE

    def in_line(j):
        return ((layer + j) % layers) * PLANE + column

    barrier = pltpu.get_barrier_semaphore()
    for j in range(1, PLANE):
        pl.semaphore_signal(barrier, inc=1, device_id={"owner": in_plane(j)}, device_id_type=MESH)
    for j in range(1, layers):
        pl.semaphore_signal(barrier, inc=1, device_id={"owner": in_line(j)}, device_id_type=MESH)
    across = {"groups": 1 - group, "owner": me}
    pl.semaphore_signal(barrier, inc=1, device_id=across, device_id_type=MESH)
    starts = slot_starts(clips_ref, me * clip_count, clip_count, clip_rows, layers, block)
    slot = lax.broadcasted_iota(jnp.int32, (slots, rows), 0)
    target = placed_rows(starts, (slots, rows), 1, clip_rows)
    place[...] = jnp.where(slot == target, 1.0, 0.0).astype(jnp.bfloat16)
    slot = lax.broadcasted_iota(jnp.int32, (rows, slots), 1)
    target = placed_rows(starts, (rows, slots), 0, clip_rows)
    unplace[...] = jnp.where(slot == target, 1.0, 0.0).astype(jnp.bfloat16)

    send_c[...] = (
        dot(place[...], cotangent_ref[...]).astype(jnp.bfloat16).reshape(send_c.shape)
    )
    pl.semaphore_wait(barrier, PLANE - 1 + layers - 1 + 1)

    def remote(src, dst, sems, at, owner):
        return pltpu.make_async_remote_copy(
            src_ref=src,
            dst_ref=dst,
            send_sem=sems.at[(0,) + at],
            recv_sem=sems.at[(1,) + at],
            device_id={"owner": owner},
            device_id_type=MESH,
        )

    def span(k):
        return pl.ds(pl.multiple_of(k * width, width), width)

    def up_copy(j):
        return remote(up_ref, all_up.at[layer], u_sem, (j,), in_line(j))

    def down_copy(k, j):
        return remote(
            down_ref.at[:, span(k)], all_down.at[k, layer], d_sem, (k, j), in_line(j)
        )

    def value_copy(j):
        return remote(
            send_c.at[(column + j) % PLANE], got_c.at[column], c_sem, (j,), in_plane(j)
        )

    def token_copy(k, j):
        return remote(
            send_t.at[k, (column + j) % PLANE], got_t.at[k, column], t_sem, (k, j), in_plane(j)
        )

    def term_copy(k, j):
        return remote(
            terms.at[k, (column + j) % PLANE], back.at[k, column], r_sem, (k, j), in_plane(j)
        )

    def grad_copy(k):
        return remote(send_g.at[k], got_g.at[k], g_sem, (k,), pair * PLANE + column)

    def far_copy(k):
        return remote(far_g.at[k], in_g.at[k], h_sem, (k,), far * PLANE + column)

    def up_grad_copy():
        return remote(send_u, got_u, v_sem, (0,), pair * PLANE + column)

    def up_far_copy():
        return remote(far_u, in_u, w_sem, (0,), far * PLANE + column)

    def hand(ref, sems, at):
        return pltpu.make_async_remote_copy(
            src_ref=ref,
            dst_ref=ref,
            send_sem=sems.at[(0,) + at],
            recv_sem=sems.at[(1,) + at],
            device_id=across,
            device_id_type=MESH,
        )

    def hand_down(k, j):
        return hand(all_down.at[k, (layer - j + layers) % layers], x_sem, (k, j))

    def hand_up(j):
        return hand(all_up.at[(layer - j + layers) % layers], y_sem, (j,))

    def pass_down(k):
        @pl.when(carrier)
        def _():
            for j in range(1, layers):
                down_copy(k, j).wait_recv()
                hand_down(k, j).start()

    @pl.when(carrier)
    def _():
        for j in range(1, layers):
            up_copy(j).start()

    for j in range(1, PLANE):
        value_copy(j).start()

    @pl.loop(0, chunks)
    def _(k):
        @pl.when(carrier)
        def _():
            for j in range(1, layers):
                down_copy(k, j).start()

        placed = dot(place[...], tokens_ref[:, span(k)]).astype(jnp.bfloat16)
        send_t[k] = placed.reshape(PLANE, block, width)
        for j in range(1, PLANE):
            token_copy(k, j).start()
        got_t[k, column] = send_t[k, column]
        all_down[k, layer] = down_ref[:, span(k)]

    got_c[column] = send_c[column]
    all_up[layer] = up_ref[...]
    frozen_copy.wait()

    @pl.loop(0, chunks)
    def _(k):
        base[k] = lax.dot_general(
            cotangent_ref[...],
            frozen[span(k), :],
            NT,
            preferred_element_type=jnp.float32,
        )

    @pl.when(carrier)
    def _():
        for j in range(1, layers):
            up_copy(j).wait_recv()
            hand_up(j).start()

    for k in range(AHEAD):
        pass_down(k)

    @pl.when(jnp.logical_not(carrier))
    def _():
        for j in range(1, layers):
            hand_up(j).wait_recv()

    for j in range(1, PLANE):
        value_copy(j).wait_recv()

    def own(shape, slot_dim, rank_dim):
        slot_layer = lax.div(
            lax.rem(lax.broadcasted_iota(jnp.int32, shape, slot_dim), block), CAP * clip_rows
        )
        return slot_layer == lax.div(lax.broadcasted_iota(jnp.int32, shape, rank_dim), rank)

    values = got_c[...].reshape(slots, got_c.shape[2])
    ups = all_up[...].reshape(all_rank, all_up.shape[2])
    full = lax.dot_general(values, ups, NT, preferred_element_type=jnp.float32)
    low[...] = jnp.where(own((slots, all_rank), 0, 1), full, 0.0).astype(jnp.bfloat16)
    full = lax.dot_general(ups, values, NT, preferred_element_type=jnp.float32)
    low_t[...] = jnp.where(own((all_rank, slots), 1, 0), full, 0.0).astype(jnp.bfloat16)
    acts[...] = jnp.zeros_like(acts)

    def send_terms(k):
        for j in range(1, PLANE):
            term_copy(k, j).start()

    def pass_grad(k):
        grad_copy(k).wait_recv()
        far_g[k] = (keep[k] + got_g[k, 1].astype(jnp.float32)).astype(jnp.bfloat16)
        far_copy(k).start()

    @pl.loop(0, chunks)
    def _(k):
        @pl.when(k + AHEAD < chunks)
        def _():
            pass_down(k + AHEAD)

        @pl.when(jnp.logical_not(carrier))
        def _():
            for j in range(1, layers):
                hand_down(k, j).wait_recv()

        downs = all_down[k].reshape(all_rank, width)
        term = dot(low[...], downs).astype(jnp.bfloat16).reshape(PLANE, block, width)
        terms[k] = term
        back[k, column] = terms[k, column]

        @pl.when(k >= HOLD)
        def _():
            send_terms(2 * (k - HOLD))
            send_terms(2 * (k - HOLD) + 1)

        for j in range(1, PLANE):
            token_copy(k, j).wait_recv()
        tokens = got_t[k].reshape(slots, width)
        grad[...] = dot(low_t[...], tokens).reshape(layers, rank, width)
        send_g[k, 0] = grad[pair].astype(jnp.bfloat16)
        send_g[k, 1] = grad[pair_far].astype(jnp.bfloat16)
        grad_copy(k).start()
        down_grad_ref[:, span(k)] = grad[layer]
        keep[k] = grad[far]
        acts[...] += lax.dot_general(downs, tokens, NT, preferred_element_type=jnp.float32)

        @pl.when(k >= LAG)
        def _():
            pass_grad(k - LAG)

    for k in range(2 * (chunks - HOLD), chunks):
        send_terms(k)

    acts_low = jnp.where(own((all_rank, slots), 1, 0), acts[...], 0.0).astype(jnp.bfloat16)
    keep_u[...] = dot(acts_low, got_c[...].reshape(slots, got_c.shape[2])).reshape(keep_u.shape)
    send_u[0] = keep_u[pair].astype(jnp.bfloat16)
    send_u[1] = keep_u[pair_far].astype(jnp.bfloat16)
    up_grad_copy().start()

    for k in range(chunks - LAG, chunks):
        pass_grad(k)
    up_grad_copy().wait_recv()
    far_u[...] = (keep_u[far] + got_u[1].astype(jnp.float32)).astype(jnp.bfloat16)
    up_far_copy().start()

    @pl.loop(0, chunks)
    def _(k):
        for j in range(1, PLANE):
            term_copy(k, j).wait_recv()
        returned = dot(unplace[...], back[k].reshape(slots, width))
        out_ref[:, span(k)] = (base[k] + returned).astype(jnp.bfloat16)

    @pl.loop(0, chunks)
    def _(k):
        far_copy(k).wait_recv()
        down_grad_ref[:, span(k)] = (
            down_grad_ref[:, span(k)]
            + got_g[k, 0].astype(jnp.float32)
            + in_g[k].astype(jnp.float32)
        )

    up_far_copy().wait_recv()
    up_grad_ref[...] = (
        keep_u[layer] + got_u[0].astype(jnp.float32) + in_u[...].astype(jnp.float32)
    )

    up_grad_copy().wait_send()
    up_far_copy().wait_send()
    for j in range(1, PLANE):
        value_copy(j).wait_send()

    @pl.when(carrier)
    def _():
        for j in range(1, layers):
            up_copy(j).wait_send()
            hand_up(j).wait_send()

    @pl.loop(0, chunks)
    def _(k):
        grad_copy(k).wait_send()
        far_copy(k).wait_send()
        for j in range(1, PLANE):
            token_copy(k, j).wait_send()
            term_copy(k, j).wait_send()

        @pl.when(carrier)
        def _():
            for j in range(1, layers):
                down_copy(k, j).wait_send()
                hand_down(k, j).wait_send()


def fused(
    tokens, cotangent, frozen_value_weight, adapter_down_weight, adapter_up_weight, speaker_of_clip
):
    owners = lax.axis_size("owner")
    layers = owners // PLANE
    clip_count = speaker_of_clip.shape[0] // owners
    rows, model_width = tokens.shape
    value_width = cotangent.shape[1]
    clip_rows = rows // clip_count
    rank = adapter_down_weight.shape[1]
    chunks = 8
    width = model_width // chunks
    block = layers * CAP * clip_rows
    slots = PLANE * block
    half = jnp.bfloat16
    vmem = pl.BlockSpec(memory_space=pltpu.VMEM)
    dma = pltpu.SemaphoreType.DMA
    out, down_grad, up_grad = pl.pallas_call(
        functools.partial(kernel, layers, clip_count, clip_rows, chunks),
        out_shape=(
            jax.ShapeDtypeStruct((rows, model_width), half),
            jax.ShapeDtypeStruct((rank, model_width), jnp.float32),
            jax.ShapeDtypeStruct((rank, value_width), jnp.float32),
        ),
        in_specs=[pl.BlockSpec(memory_space=pltpu.SMEM)]
        + [vmem] * 4
        + [pl.BlockSpec(memory_space=pl.ANY)],
        out_specs=(vmem, vmem, vmem),
        scratch_shapes=[
            pltpu.VMEM((model_width, value_width), half),
            pltpu.VMEM((slots, rows), half),
            pltpu.VMEM((rows, slots), half),
            pltpu.VMEM((chunks, PLANE, block, width), half),
            pltpu.VMEM((PLANE, block, value_width), half),
            pltpu.VMEM((chunks, PLANE, block, width), half),
            pltpu.VMEM((PLANE, block, value_width), half),
            pltpu.VMEM((chunks, layers, rank, width), half),
            pltpu.VMEM((layers, rank, value_width), half),
            pltpu.VMEM((slots, layers * rank), half),
            pltpu.VMEM((layers * rank, slots), half),
            pltpu.VMEM((layers * rank, slots), jnp.float32),
            pltpu.VMEM((chunks, PLANE, block, width), half),
            pltpu.VMEM((chunks, PLANE, block, width), half),
            pltpu.VMEM((layers, rank, width), jnp.float32),
            pltpu.VMEM((chunks, rank, width), jnp.float32),
            pltpu.VMEM((chunks, 2, rank, width), half),
            pltpu.VMEM((chunks, 2, rank, width), half),
            pltpu.VMEM((chunks, rank, width), half),
            pltpu.VMEM((chunks, rank, width), half),
            pltpu.VMEM((layers, rank, value_width), jnp.float32),
            pltpu.VMEM((2, rank, value_width), half),
            pltpu.VMEM((2, rank, value_width), half),
            pltpu.VMEM((rank, value_width), half),
            pltpu.VMEM((rank, value_width), half),
            pltpu.VMEM((chunks, rows, width), jnp.float32),
            dma(()),
            dma((2, chunks, PLANE)),
            dma((2, PLANE)),
            dma((2, chunks, layers)),
            dma((2, layers)),
            dma((2, chunks, PLANE)),
            dma((2, chunks)),
            dma((2, chunks)),
            dma((2, 1)),
            dma((2, 1)),
            dma((2, chunks, layers)),
            dma((2, layers)),
        ],
        compiler_params=pltpu.CompilerParams(
            collective_id=0, has_side_effects=True, vmem_limit_bytes=56 * 2**20
        ),
        cost_estimate=pl.CostEstimate(
            flops=8 * 10**9, bytes_accessed=16 * 2**20, transcendentals=0
        ),
    )(
        speaker_of_clip,
        tokens,
        cotangent,
        adapter_down_weight[0],
        adapter_up_weight[0],
        frozen_value_weight,
    )
    return out, down_grad[None], up_grad[None]


def solution(mesh):
    sizes = [mesh.shape[axis] for axis in ("groups", "owner", "tensor")]
    body = fused if sizes == [2, 16, 1] else shards
    return jax.shard_map(
        body,
        mesh=mesh,
        in_specs=(
            P(("groups", "owner"), "tensor"),
            P(("groups", "owner"), None),
            P("tensor", None),
            P("owner", None, "tensor"),
            P("owner", None, "tensor"),
            P("groups"),
        ),
        out_specs=(
            P(("groups", "owner"), "tensor"),
            P(("groups", "owner"), None, "tensor"),
            P(("groups", "owner"), None, "tensor"),
        ),
        check_vma=False,
    )
```

```python
import functools

import jax
import jax.numpy as jnp
from jax import lax
from jax.experimental import pallas as pl
from jax.experimental.pallas import tpu as pltpu
from jax.sharding import PartitionSpec as P

CAP = 2


def shards(
    tokens, cotangent, frozen_value_weight, adapter_down_weight, adapter_up_weight, speaker_of_clip
):
    owners = lax.axis_size("owner")
    my_index = lax.axis_index("owner")
    core_index = lax.axis_index("tensor")
    clip_count = speaker_of_clip.shape[0] // owners
    clip_rows = tokens.shape[0] // clip_count
    model_width_half = tokens.shape[1]
    value_width_half = adapter_up_weight.shape[2]
    slot_count = owners * CAP
    contract_last = (((1,), (1,)), ((), ()))
    contract_leading = (((0,), (0,)), ((), ()))
    my_clips = lax.dynamic_slice_in_dim(speaker_of_clip, my_index * clip_count, clip_count)
    clip_order = jnp.arange(clip_count)
    earlier = (my_clips[:, None] == my_clips[None, :]) & (clip_order[None, :] < clip_order[:, None])
    position = jnp.sum(earlier.astype(jnp.int32), axis=1)
    target = my_clips * CAP + position
    placing = (jnp.arange(slot_count)[:, None] == target[None, :]).astype(jnp.bfloat16)
    value_rows = lax.dynamic_slice_in_dim(
        cotangent, core_index * value_width_half, value_width_half, 1
    )
    send_tokens = jnp.dot(
        placing, tokens.reshape(clip_count, -1), preferred_element_type=jnp.float32
    )
    send_tokens = send_tokens.astype(jnp.bfloat16).reshape(
        owners, CAP * clip_rows, model_width_half
    )
    send_values = jnp.dot(
        placing, value_rows.reshape(clip_count, -1), preferred_element_type=jnp.float32
    )
    send_values = send_values.astype(jnp.bfloat16).reshape(
        owners, CAP * clip_rows, value_width_half
    )
    got_tokens, got_values = (
        lax.all_to_all(send_tokens, "owner", split_axis=0, concat_axis=0, tiled=True),
        lax.all_to_all(send_values, "owner", split_axis=0, concat_axis=0, tiled=True),
    )
    in_rows = got_tokens.reshape(-1, model_width_half)
    in_values = got_values.reshape(-1, value_width_half)
    down_gradient_local = adapter_down_weight[0]
    up_gradient_local = adapter_up_weight[0]
    acts_part = lax.dot_general(
        down_gradient_local, in_rows, contract_last, preferred_element_type=jnp.float32
    )
    back_part = lax.dot_general(
        up_gradient_local, in_values, contract_last, preferred_element_type=jnp.float32
    )
    acts_sum, back_sum = lax.psum((acts_part, back_part), "tensor")
    acts_low = acts_sum.astype(jnp.bfloat16)
    low_rank_gradient = back_sum.astype(jnp.bfloat16)
    down_grad = jnp.dot(low_rank_gradient, in_rows, preferred_element_type=jnp.float32)[None]
    up_grad = jnp.dot(acts_low, in_values, preferred_element_type=jnp.float32)[None]
    frozen_gradient = lax.dot_general(
        cotangent, frozen_value_weight, contract_last, preferred_element_type=jnp.float32
    )
    slot_terms = lax.dot_general(
        low_rank_gradient, down_gradient_local, contract_leading, preferred_element_type=jnp.float32
    )
    slot_terms = slot_terms.astype(jnp.bfloat16).reshape(owners, CAP * clip_rows, model_width_half)
    returned = lax.all_to_all(slot_terms, "owner", split_axis=0, concat_axis=0, tiled=True)
    adapter_gradient = lax.dot_general(
        placing,
        returned.reshape(slot_count, -1),
        contract_leading,
        preferred_element_type=jnp.float32,
    )
    adapter_gradient = adapter_gradient.reshape(-1, model_width_half)
    input_row_gradient = (frozen_gradient + adapter_gradient).astype(jnp.bfloat16)
    return (input_row_gradient, down_grad, up_grad)


PLANE = 4
AHEAD = 2
LAG = 2
HOLD = 5
MESH = pl.DeviceIdType.MESH
NT = (((1,), (1,)), ((), ()))


def dot(a, b):
    return jnp.dot(a, b, preferred_element_type=jnp.float32)


def slot_starts(clips_ref, first, clip_count, clip_rows, layers, block):
    speakers = [clips_ref[first + j] for j in range(clip_count)]
    starts = []
    for j in range(clip_count):
        position = jnp.int32(0)
        for i in range(j):
            position = position + jnp.where(speakers[i] == speakers[j], 1, 0)
        speaker = speakers[j]
        column = lax.rem(speaker, PLANE)
        layer = lax.div(speaker, PLANE)
        starts.append(column * block + layer * (CAP * clip_rows) + position * clip_rows)
    return starts


def placed_rows(starts, shape, dim, clip_rows):
    token = lax.broadcasted_iota(jnp.int32, shape, dim)
    clip = lax.div(token, clip_rows)
    target = lax.rem(token, clip_rows)
    for j, start in enumerate(starts):
        target = target + jnp.where(clip == j, start, 0)
    return target


def kernel(
    layers,
    clip_count,
    clip_rows,
    chunks,
    clips_ref,
    tokens_hbm,
    cotangent_ref,
    down_hbm,
    up_ref,
    frozen_ref,
    out_hbm,
    down_grad_hbm,
    up_grad_hbm,
    tokens_ref,
    down_ref,
    out_ref,
    down_grad_ref,
    up_grad_ref,
    frozen,
    place,
    unplace,
    send_t,
    send_c,
    got_t,
    got_c,
    all_down,
    all_up,
    low,
    low_t,
    acts,
    terms,
    back,
    grad,
    keep,
    send_g,
    got_g,
    far_g,
    in_g,
    keep_u,
    send_u,
    got_u,
    far_u,
    in_u,
    base,
    in_sem,
    out_sem,
    grad_sem,
    up_out_sem,
    frozen_sem,
    t_sem,
    c_sem,
    d_sem,
    u_sem,
    r_sem,
    g_sem,
    h_sem,
    v_sem,
    w_sem,
    x_sem,
    y_sem,
):
    me = lax.axis_index("owner")
    group = lax.axis_index("groups")
    column = me % PLANE
    layer = me // PLANE
    carrier = column % 2 == group
    pair = layer + 1 - 2 * (layer % 2)
    far = (layer + 2) % layers
    pair_far = (pair + 2) % layers
    rows = tokens_ref.shape[0]
    width = tokens_ref.shape[1] // chunks
    rank = down_ref.shape[0]
    block = layers * CAP * clip_rows
    slots = PLANE * block
    all_rank = layers * rank

    frozen_copy = pltpu.make_async_copy(frozen_ref, frozen, frozen_sem)
    tokens_in = pltpu.make_async_copy(tokens_hbm, tokens_ref, in_sem.at[0])
    down_in = pltpu.make_async_copy(down_hbm, down_ref, in_sem.at[1])
    tokens_in.start()
    down_in.start()

    def in_plane(j):
        return layer * PLANE + (column + j) % PLANE

    def in_line(j):
        return ((layer + j) % layers) * PLANE + column

    barrier = pltpu.get_barrier_semaphore()
    for j in range(1, PLANE):
        pl.semaphore_signal(barrier, inc=1, device_id={"owner": in_plane(j)}, device_id_type=MESH)
    for j in range(1, layers):
        pl.semaphore_signal(barrier, inc=1, device_id={"owner": in_line(j)}, device_id_type=MESH)
    across = {"groups": 1 - group, "owner": me}
    pl.semaphore_signal(barrier, inc=1, device_id=across, device_id_type=MESH)
    starts = slot_starts(clips_ref, me * clip_count, clip_count, clip_rows, layers, block)
    slot = lax.broadcasted_iota(jnp.int32, (slots, rows), 0)
    target = placed_rows(starts, (slots, rows), 1, clip_rows)
    place[...] = jnp.where(slot == target, 1.0, 0.0).astype(jnp.bfloat16)

    send_c[...] = (
        dot(place[...], cotangent_ref[...]).astype(jnp.bfloat16).reshape(send_c.shape)
    )
    pl.semaphore_wait(barrier, PLANE - 1 + layers - 1 + 1)

    def remote(src, dst, sems, at, owner):
        return pltpu.make_async_remote_copy(
            src_ref=src,
            dst_ref=dst,
            send_sem=sems.at[(0,) + at],
            recv_sem=sems.at[(1,) + at],
            device_id={"owner": owner},
            device_id_type=MESH,
        )

    def span(k):
        return pl.ds(pl.multiple_of(k * width, width), width)

    def up_copy(j):
        return remote(up_ref, all_up.at[layer], u_sem, (j,), in_line(j))

    def down_copy(k, j):
        return remote(
            down_ref.at[:, span(k)], all_down.at[k, layer], d_sem, (k, j), in_line(j)
        )

    def value_copy(j):
        return remote(
            send_c.at[(column + j) % PLANE], got_c.at[column], c_sem, (j,), in_plane(j)
        )

    def token_copy(k, j):
        return remote(
            send_t.at[k, (column + j) % PLANE], got_t.at[k, column], t_sem, (k, j), in_plane(j)
        )

    def term_copy(k, j):
        return remote(
            terms.at[k, (column + j) % PLANE], back.at[k, column], r_sem, (k, j), in_plane(j)
        )

    def grad_copy(k):
        return remote(send_g.at[k], got_g.at[k], g_sem, (k,), pair * PLANE + column)

    def far_copy(k):
        return remote(far_g.at[k], in_g.at[k], h_sem, (k,), far * PLANE + column)

    def up_grad_copy():
        return remote(send_u, got_u, v_sem, (0,), pair * PLANE + column)

    def up_far_copy():
        return remote(far_u, in_u, w_sem, (0,), far * PLANE + column)

    def hand(ref, sems, at):
        return pltpu.make_async_remote_copy(
            src_ref=ref,
            dst_ref=ref,
            send_sem=sems.at[(0,) + at],
            recv_sem=sems.at[(1,) + at],
            device_id=across,
            device_id_type=MESH,
        )

    def hand_down(k, j):
        return hand(all_down.at[k, (layer - j + layers) % layers], x_sem, (k, j))

    def hand_up(j):
        return hand(all_up.at[(layer - j + layers) % layers], y_sem, (j,))

    def pass_down(k):
        @pl.when(carrier)
        def _():
            for j in range(1, layers):
                down_copy(k, j).wait_recv()
                hand_down(k, j).start()

    @pl.when(carrier)
    def _():
        for j in range(1, layers):
            up_copy(j).start()

    for j in range(1, PLANE):
        value_copy(j).start()

    tokens_in.wait()
    down_in.wait()
    frozen_copy.start()

    @pl.loop(0, chunks)
    def _(k):
        @pl.when(carrier)
        def _():
            for j in range(1, layers):
                down_copy(k, j).start()

        placed = dot(place[...], tokens_ref[:, span(k)]).astype(jnp.bfloat16)
        send_t[k] = placed.reshape(PLANE, block, width)
        for j in range(1, PLANE):
            token_copy(k, j).start()
        got_t[k, column] = send_t[k, column]
        all_down[k, layer] = down_ref[:, span(k)]

    slot = lax.broadcasted_iota(jnp.int32, (rows, slots), 1)
    target = placed_rows(starts, (rows, slots), 0, clip_rows)
    unplace[...] = jnp.where(slot == target, 1.0, 0.0).astype(jnp.bfloat16)
    got_c[column] = send_c[column]
    all_up[layer] = up_ref[...]
    frozen_copy.wait()

    @pl.loop(0, chunks)
    def _(k):
        base[k] = lax.dot_general(
            cotangent_ref[...],
            frozen[span(k), :],
            NT,
            preferred_element_type=jnp.float32,
        )

    @pl.when(carrier)
    def _():
        for j in range(1, layers):
            up_copy(j).wait_recv()
            hand_up(j).start()

    for k in range(AHEAD):
        pass_down(k)

    @pl.when(jnp.logical_not(carrier))
    def _():
        for j in range(1, layers):
            hand_up(j).wait_recv()

    for j in range(1, PLANE):
        value_copy(j).wait_recv()

    def own(shape, slot_dim, rank_dim):
        slot_layer = lax.div(
            lax.rem(lax.broadcasted_iota(jnp.int32, shape, slot_dim), block), CAP * clip_rows
        )
        return slot_layer == lax.div(lax.broadcasted_iota(jnp.int32, shape, rank_dim), rank)

    values = got_c[...].reshape(slots, got_c.shape[2])
    ups = all_up[...].reshape(all_rank, all_up.shape[2])
    full = lax.dot_general(values, ups, NT, preferred_element_type=jnp.float32)
    low[...] = jnp.where(own((slots, all_rank), 0, 1), full, 0.0).astype(jnp.bfloat16)
    full = lax.dot_general(ups, values, NT, preferred_element_type=jnp.float32)
    low_t[...] = jnp.where(own((all_rank, slots), 1, 0), full, 0.0).astype(jnp.bfloat16)
    acts[...] = jnp.zeros_like(acts)

    def send_terms(k):
        for j in range(1, PLANE):
            term_copy(k, j).start()

    def pass_grad(k):
        grad_copy(k).wait_recv()
        far_g[k] = (keep[k] + got_g[k, 1].astype(jnp.float32)).astype(jnp.bfloat16)
        far_copy(k).start()

    @pl.loop(0, chunks)
    def _(k):
        @pl.when(k + AHEAD < chunks)
        def _():
            pass_down(k + AHEAD)

        @pl.when(jnp.logical_not(carrier))
        def _():
            for j in range(1, layers):
                hand_down(k, j).wait_recv()

        downs = all_down[k].reshape(all_rank, width)
        term = dot(low[...], downs).astype(jnp.bfloat16).reshape(PLANE, block, width)
        terms[k] = term
        back[k, column] = terms[k, column]

        @pl.when(k >= HOLD)
        def _():
            send_terms(2 * (k - HOLD))
            send_terms(2 * (k - HOLD) + 1)

        for j in range(1, PLANE):
            token_copy(k, j).wait_recv()
        tokens = got_t[k].reshape(slots, width)
        grad[...] = dot(low_t[...], tokens).reshape(layers, rank, width)
        send_g[k, 0] = grad[pair].astype(jnp.bfloat16)
        send_g[k, 1] = grad[pair_far].astype(jnp.bfloat16)
        grad_copy(k).start()
        down_grad_ref[:, span(k)] = grad[layer]
        keep[k] = grad[far]
        acts[...] += lax.dot_general(downs, tokens, NT, preferred_element_type=jnp.float32)

        @pl.when(k >= LAG)
        def _():
            pass_grad(k - LAG)

    for k in range(2 * (chunks - HOLD), chunks):
        send_terms(k)

    acts_low = jnp.where(own((all_rank, slots), 1, 0), acts[...], 0.0).astype(jnp.bfloat16)
    keep_u[...] = dot(acts_low, got_c[...].reshape(slots, got_c.shape[2])).reshape(keep_u.shape)
    send_u[0] = keep_u[pair].astype(jnp.bfloat16)
    send_u[1] = keep_u[pair_far].astype(jnp.bfloat16)
    up_grad_copy().start()

    for k in range(chunks - LAG, chunks):
        pass_grad(k)
    up_grad_copy().wait_recv()
    far_u[...] = (keep_u[far] + got_u[1].astype(jnp.float32)).astype(jnp.bfloat16)
    up_far_copy().start()

    def row_out(k):
        return pltpu.make_async_copy(
            out_ref.at[:, span(k)], out_hbm.at[:, span(k)], out_sem.at[k]
        )

    def grad_out(k):
        return pltpu.make_async_copy(
            down_grad_ref.at[:, span(k)], down_grad_hbm.at[:, span(k)], grad_sem.at[k]
        )

    up_out = pltpu.make_async_copy(up_grad_ref, up_grad_hbm, up_out_sem)

    @pl.loop(0, chunks)
    def _(k):
        far_copy(k).wait_recv()
        down_grad_ref[:, span(k)] = (
            down_grad_ref[:, span(k)]
            + got_g[k, 0].astype(jnp.float32)
            + in_g[k].astype(jnp.float32)
        )
        grad_out(k).start()

    up_far_copy().wait_recv()
    up_grad_ref[...] = (
        keep_u[layer] + got_u[0].astype(jnp.float32) + in_u[...].astype(jnp.float32)
    )
    up_out.start()

    @pl.loop(0, chunks)
    def _(k):
        for j in range(1, PLANE):
            term_copy(k, j).wait_recv()
        returned = dot(unplace[...], back[k].reshape(slots, width))
        out_ref[:, span(k)] = (base[k] + returned).astype(jnp.bfloat16)
        row_out(k).start()

    up_out.wait()
    up_grad_copy().wait_send()
    up_far_copy().wait_send()
    for j in range(1, PLANE):
        value_copy(j).wait_send()

    @pl.when(carrier)
    def _():
        for j in range(1, layers):
            up_copy(j).wait_send()
            hand_up(j).wait_send()

    @pl.loop(0, chunks)
    def _(k):
        row_out(k).wait()
        grad_out(k).wait()
        grad_copy(k).wait_send()
        far_copy(k).wait_send()
        for j in range(1, PLANE):
            token_copy(k, j).wait_send()
            term_copy(k, j).wait_send()

        @pl.when(carrier)
        def _():
            for j in range(1, layers):
                down_copy(k, j).wait_send()
                hand_down(k, j).wait_send()


def fused(
    tokens, cotangent, frozen_value_weight, adapter_down_weight, adapter_up_weight, speaker_of_clip
):
    owners = lax.axis_size("owner")
    layers = owners // PLANE
    clip_count = speaker_of_clip.shape[0] // owners
    rows, model_width = tokens.shape
    value_width = cotangent.shape[1]
    clip_rows = rows // clip_count
    rank = adapter_down_weight.shape[1]
    chunks = 8
    width = model_width // chunks
    block = layers * CAP * clip_rows
    slots = PLANE * block
    half = jnp.bfloat16
    vmem = pl.BlockSpec(memory_space=pltpu.VMEM)
    anywhere = pl.BlockSpec(memory_space=pl.ANY)
    dma = pltpu.SemaphoreType.DMA
    out, down_grad, up_grad = pl.pallas_call(
        functools.partial(kernel, layers, clip_count, clip_rows, chunks),
        out_shape=(
            jax.ShapeDtypeStruct((rows, model_width), half),
            jax.ShapeDtypeStruct((rank, model_width), jnp.float32),
            jax.ShapeDtypeStruct((rank, value_width), jnp.float32),
        ),
        in_specs=[pl.BlockSpec(memory_space=pltpu.SMEM), anywhere, vmem, anywhere, vmem, anywhere],
        out_specs=(anywhere, anywhere, anywhere),
        scratch_shapes=[
            pltpu.VMEM((rows, model_width), half),
            pltpu.VMEM((rank, model_width), half),
            pltpu.VMEM((rows, model_width), half),
            pltpu.VMEM((rank, model_width), jnp.float32),
            pltpu.VMEM((rank, value_width), jnp.float32),
            pltpu.VMEM((model_width, value_width), half),
            pltpu.VMEM((slots, rows), half),
            pltpu.VMEM((rows, slots), half),
            pltpu.VMEM((chunks, PLANE, block, width), half),
            pltpu.VMEM((PLANE, block, value_width), half),
            pltpu.VMEM((chunks, PLANE, block, width), half),
            pltpu.VMEM((PLANE, block, value_width), half),
            pltpu.VMEM((chunks, layers, rank, width), half),
            pltpu.VMEM((layers, rank, value_width), half),
            pltpu.VMEM((slots, layers * rank), half),
            pltpu.VMEM((layers * rank, slots), half),
            pltpu.VMEM((layers * rank, slots), jnp.float32),
            pltpu.VMEM((chunks, PLANE, block, width), half),
            pltpu.VMEM((chunks, PLANE, block, width), half),
            pltpu.VMEM((layers, rank, width), jnp.float32),
            pltpu.VMEM((chunks, rank, width), jnp.float32),
            pltpu.VMEM((chunks, 2, rank, width), half),
            pltpu.VMEM((chunks, 2, rank, width), half),
            pltpu.VMEM((chunks, rank, width), half),
            pltpu.VMEM((chunks, rank, width), half),
            pltpu.VMEM((layers, rank, value_width), jnp.float32),
            pltpu.VMEM((2, rank, value_width), half),
            pltpu.VMEM((2, rank, value_width), half),
            pltpu.VMEM((rank, value_width), half),
            pltpu.VMEM((rank, value_width), half),
            pltpu.VMEM((chunks, rows, width), jnp.float32),
            dma((2,)),
            dma((chunks,)),
            dma((chunks,)),
            dma(()),
            dma(()),
            dma((2, chunks, PLANE)),
            dma((2, PLANE)),
            dma((2, chunks, layers)),
            dma((2, layers)),
            dma((2, chunks, PLANE)),
            dma((2, chunks)),
            dma((2, chunks)),
            dma((2, 1)),
            dma((2, 1)),
            dma((2, chunks, layers)),
            dma((2, layers)),
        ],
        compiler_params=pltpu.CompilerParams(
            collective_id=0, has_side_effects=True, vmem_limit_bytes=56 * 2**20
        ),
        cost_estimate=pl.CostEstimate(
            flops=8 * 10**9, bytes_accessed=16 * 2**20, transcendentals=0
        ),
    )(
        speaker_of_clip,
        tokens,
        cotangent,
        adapter_down_weight[0],
        adapter_up_weight[0],
        frozen_value_weight,
    )
    return out, down_grad[None], up_grad[None]


def solution(mesh):
    sizes = [mesh.shape[axis] for axis in ("groups", "owner", "tensor")]
    body = fused if sizes == [2, 16, 1] else shards
    return jax.shard_map(
        body,
        mesh=mesh,
        in_specs=(
            P(("groups", "owner"), "tensor"),
            P(("groups", "owner"), None),
            P("tensor", None),
            P("owner", None, "tensor"),
            P("owner", None, "tensor"),
            P("groups"),
        ),
        out_specs=(
            P(("groups", "owner"), "tensor"),
            P(("groups", "owner"), None, "tensor"),
            P(("groups", "owner"), None, "tensor"),
        ),
        check_vma=False,
    )
```

```python
import functools

import jax
import jax.numpy as jnp
from jax import lax
from jax.experimental import pallas as pl
from jax.experimental.pallas import tpu as pltpu
from jax.sharding import PartitionSpec as P

CAP = 2


def shards(
    tokens, cotangent, frozen_value_weight, adapter_down_weight, adapter_up_weight, speaker_of_clip
):
    owners = lax.axis_size("owner")
    my_index = lax.axis_index("owner")
    core_index = lax.axis_index("tensor")
    clip_count = speaker_of_clip.shape[0] // owners
    clip_rows = tokens.shape[0] // clip_count
    model_width_half = tokens.shape[1]
    value_width_half = adapter_up_weight.shape[2]
    slot_count = owners * CAP
    contract_last = (((1,), (1,)), ((), ()))
    contract_leading = (((0,), (0,)), ((), ()))
    my_clips = lax.dynamic_slice_in_dim(speaker_of_clip, my_index * clip_count, clip_count)
    clip_order = jnp.arange(clip_count)
    earlier = (my_clips[:, None] == my_clips[None, :]) & (clip_order[None, :] < clip_order[:, None])
    position = jnp.sum(earlier.astype(jnp.int32), axis=1)
    target = my_clips * CAP + position
    placing = (jnp.arange(slot_count)[:, None] == target[None, :]).astype(jnp.bfloat16)
    value_rows = lax.dynamic_slice_in_dim(
        cotangent, core_index * value_width_half, value_width_half, 1
    )
    send_tokens = jnp.dot(
        placing, tokens.reshape(clip_count, -1), preferred_element_type=jnp.float32
    )
    send_tokens = send_tokens.astype(jnp.bfloat16).reshape(
        owners, CAP * clip_rows, model_width_half
    )
    send_values = jnp.dot(
        placing, value_rows.reshape(clip_count, -1), preferred_element_type=jnp.float32
    )
    send_values = send_values.astype(jnp.bfloat16).reshape(
        owners, CAP * clip_rows, value_width_half
    )
    got_tokens, got_values = (
        lax.all_to_all(send_tokens, "owner", split_axis=0, concat_axis=0, tiled=True),
        lax.all_to_all(send_values, "owner", split_axis=0, concat_axis=0, tiled=True),
    )
    in_rows = got_tokens.reshape(-1, model_width_half)
    in_values = got_values.reshape(-1, value_width_half)
    down_gradient_local = adapter_down_weight[0]
    up_gradient_local = adapter_up_weight[0]
    acts_part = lax.dot_general(
        down_gradient_local, in_rows, contract_last, preferred_element_type=jnp.float32
    )
    back_part = lax.dot_general(
        up_gradient_local, in_values, contract_last, preferred_element_type=jnp.float32
    )
    acts_sum, back_sum = lax.psum((acts_part, back_part), "tensor")
    acts_low = acts_sum.astype(jnp.bfloat16)
    low_rank_gradient = back_sum.astype(jnp.bfloat16)
    down_grad = jnp.dot(low_rank_gradient, in_rows, preferred_element_type=jnp.float32)[None]
    up_grad = jnp.dot(acts_low, in_values, preferred_element_type=jnp.float32)[None]
    frozen_gradient = lax.dot_general(
        cotangent, frozen_value_weight, contract_last, preferred_element_type=jnp.float32
    )
    slot_terms = lax.dot_general(
        low_rank_gradient, down_gradient_local, contract_leading, preferred_element_type=jnp.float32
    )
    slot_terms = slot_terms.astype(jnp.bfloat16).reshape(owners, CAP * clip_rows, model_width_half)
    returned = lax.all_to_all(slot_terms, "owner", split_axis=0, concat_axis=0, tiled=True)
    adapter_gradient = lax.dot_general(
        placing,
        returned.reshape(slot_count, -1),
        contract_leading,
        preferred_element_type=jnp.float32,
    )
    adapter_gradient = adapter_gradient.reshape(-1, model_width_half)
    input_row_gradient = (frozen_gradient + adapter_gradient).astype(jnp.bfloat16)
    return (input_row_gradient, down_grad, up_grad)


PLANE = 4
AHEAD = 2
LAG = 1
HOLD = 2
MESH = pl.DeviceIdType.MESH
NT = (((1,), (1,)), ((), ()))


def dot(a, b):
    return jnp.dot(a, b, preferred_element_type=jnp.float32)


def slot_starts(clips_ref, first, clip_count, clip_rows, layers, block):
    speakers = [clips_ref[first + j] for j in range(clip_count)]
    starts = []
    for j in range(clip_count):
        position = jnp.int32(0)
        for i in range(j):
            position = position + jnp.where(speakers[i] == speakers[j], 1, 0)
        speaker = speakers[j]
        column = lax.rem(speaker, PLANE)
        layer = lax.div(speaker, PLANE)
        starts.append(column * block + layer * (CAP * clip_rows) + position * clip_rows)
    return starts


def placed_rows(starts, shape, dim, clip_rows):
    token = lax.broadcasted_iota(jnp.int32, shape, dim)
    clip = lax.div(token, clip_rows)
    target = lax.rem(token, clip_rows)
    for j, start in enumerate(starts):
        target = target + jnp.where(clip == j, start, 0)
    return target


def kernel(
    layers,
    clip_count,
    clip_rows,
    chunks,
    clips_ref,
    tokens_hbm,
    cotangent_ref,
    down_hbm,
    up_ref,
    frozen_ref,
    out_hbm,
    down_grad_hbm,
    up_grad_hbm,
    tokens_ref,
    down_ref,
    out_ref,
    down_grad_ref,
    up_grad_ref,
    frozen,
    place,
    unplace,
    send_t,
    send_c,
    got_t,
    got_c,
    all_down,
    all_up,
    low,
    low_t,
    acts,
    terms,
    back,
    grad,
    keep,
    send_g,
    got_g,
    far_g,
    in_g,
    keep_u,
    send_u,
    got_u,
    far_u,
    in_u,
    base,
    in_sem,
    out_sem,
    grad_sem,
    up_out_sem,
    frozen_sem,
    t_sem,
    c_sem,
    d_sem,
    u_sem,
    r_sem,
    g_sem,
    h_sem,
    v_sem,
    w_sem,
    x_sem,
    y_sem,
):
    me = lax.axis_index("owner")
    group = lax.axis_index("groups")
    column = me % PLANE
    layer = me // PLANE
    carrier = column % 2 == group
    pair = layer + 1 - 2 * (layer % 2)
    far = (layer + 2) % layers
    pair_far = (pair + 2) % layers
    rows = tokens_ref.shape[0]
    width = tokens_ref.shape[1] // chunks
    rank = down_ref.shape[0]
    block = layers * CAP * clip_rows
    slots = PLANE * block
    all_rank = layers * rank

    frozen_copy = pltpu.make_async_copy(frozen_ref, frozen, frozen_sem)
    tokens_in = pltpu.make_async_copy(tokens_hbm, tokens_ref, in_sem.at[0])
    down_in = pltpu.make_async_copy(down_hbm, down_ref, in_sem.at[1])
    tokens_in.start()
    down_in.start()

    def in_plane(j):
        return layer * PLANE + (column + j) % PLANE

    def in_line(j):
        return ((layer + j) % layers) * PLANE + column

    barrier = pltpu.get_barrier_semaphore()
    for j in range(1, PLANE):
        pl.semaphore_signal(barrier, inc=1, device_id={"owner": in_plane(j)}, device_id_type=MESH)
    for j in range(1, layers):
        pl.semaphore_signal(barrier, inc=1, device_id={"owner": in_line(j)}, device_id_type=MESH)
    across = {"groups": 1 - group, "owner": me}
    pl.semaphore_signal(barrier, inc=1, device_id=across, device_id_type=MESH)
    starts = slot_starts(clips_ref, me * clip_count, clip_count, clip_rows, layers, block)
    slot = lax.broadcasted_iota(jnp.int32, (slots, rows), 0)
    target = placed_rows(starts, (slots, rows), 1, clip_rows)
    place[...] = jnp.where(slot == target, 1.0, 0.0).astype(jnp.bfloat16)

    send_c[...] = (
        dot(place[...], cotangent_ref[...]).astype(jnp.bfloat16).reshape(send_c.shape)
    )
    pl.semaphore_wait(barrier, PLANE - 1 + layers - 1 + 1)

    def remote(src, dst, sems, at, owner):
        return pltpu.make_async_remote_copy(
            src_ref=src,
            dst_ref=dst,
            send_sem=sems.at[(0,) + at],
            recv_sem=sems.at[(1,) + at],
            device_id={"owner": owner},
            device_id_type=MESH,
        )

    def span(k):
        return pl.ds(pl.multiple_of(k * width, width), width)

    def up_copy(j):
        return remote(up_ref, all_up.at[layer], u_sem, (j,), in_line(j))

    def down_copy(k, j):
        return remote(
            down_ref.at[:, span(k)], all_down.at[k, layer], d_sem, (k, j), in_line(j)
        )

    def value_copy(j):
        return remote(
            send_c.at[(column + j) % PLANE], got_c.at[column], c_sem, (j,), in_plane(j)
        )

    def token_copy(k, j):
        return remote(
            send_t.at[k, (column + j) % PLANE], got_t.at[k, column], t_sem, (k, j), in_plane(j)
        )

    def term_copy(k, j):
        return remote(
            terms.at[k, (column + j) % PLANE], back.at[k, column], r_sem, (k, j), in_plane(j)
        )

    def grad_copy(k):
        return remote(send_g.at[k], got_g.at[k], g_sem, (k,), pair * PLANE + column)

    def far_copy(k):
        return remote(far_g.at[k], in_g.at[k], h_sem, (k,), far * PLANE + column)

    def up_grad_copy():
        return remote(send_u, got_u, v_sem, (0,), pair * PLANE + column)

    def up_far_copy():
        return remote(far_u, in_u, w_sem, (0,), far * PLANE + column)

    def hand(ref, sems, at):
        return pltpu.make_async_remote_copy(
            src_ref=ref,
            dst_ref=ref,
            send_sem=sems.at[(0,) + at],
            recv_sem=sems.at[(1,) + at],
            device_id=across,
            device_id_type=MESH,
        )

    def hand_down(k, j):
        return hand(all_down.at[k, (layer - j + layers) % layers], x_sem, (k, j))

    def hand_up(j):
        return hand(all_up.at[(layer - j + layers) % layers], y_sem, (j,))

    def pass_down(k):
        @pl.when(carrier)
        def _():
            for j in range(1, layers):
                down_copy(k, j).wait_recv()
                hand_down(k, j).start()

    @pl.when(carrier)
    def _():
        for j in range(1, layers):
            up_copy(j).start()

    for j in range(1, PLANE):
        value_copy(j).start()

    tokens_in.wait()
    down_in.wait()
    frozen_copy.start()

    @pl.loop(0, chunks)
    def _(k):
        @pl.when(carrier)
        def _():
            for j in range(1, layers):
                down_copy(k, j).start()

        placed = dot(place[...], tokens_ref[:, span(k)]).astype(jnp.bfloat16)
        send_t[k] = placed.reshape(PLANE, block, width)
        for j in range(1, PLANE):
            token_copy(k, j).start()
        got_t[k, column] = send_t[k, column]
        all_down[k, layer] = down_ref[:, span(k)]

    slot = lax.broadcasted_iota(jnp.int32, (rows, slots), 1)
    target = placed_rows(starts, (rows, slots), 0, clip_rows)
    unplace[...] = jnp.where(slot == target, 1.0, 0.0).astype(jnp.bfloat16)
    got_c[column] = send_c[column]
    all_up[layer] = up_ref[...]
    frozen_copy.wait()

    @pl.loop(0, chunks)
    def _(k):
        base[k] = lax.dot_general(
            cotangent_ref[...],
            frozen[span(k), :],
            NT,
            preferred_element_type=jnp.float32,
        )

    @pl.when(carrier)
    def _():
        for j in range(1, layers):
            up_copy(j).wait_recv()
            hand_up(j).start()

    for k in range(AHEAD):
        pass_down(k)

    @pl.when(jnp.logical_not(carrier))
    def _():
        for j in range(1, layers):
            hand_up(j).wait_recv()

    for j in range(1, PLANE):
        value_copy(j).wait_recv()

    def own(shape, slot_dim, rank_dim):
        slot_layer = lax.div(
            lax.rem(lax.broadcasted_iota(jnp.int32, shape, slot_dim), block), CAP * clip_rows
        )
        return slot_layer == lax.div(lax.broadcasted_iota(jnp.int32, shape, rank_dim), rank)

    values = got_c[...].reshape(slots, got_c.shape[2])
    ups = all_up[...].reshape(all_rank, all_up.shape[2])
    full = lax.dot_general(values, ups, NT, preferred_element_type=jnp.float32)
    low[...] = jnp.where(own((slots, all_rank), 0, 1), full, 0.0).astype(jnp.bfloat16)
    full = lax.dot_general(ups, values, NT, preferred_element_type=jnp.float32)
    low_t[...] = jnp.where(own((all_rank, slots), 1, 0), full, 0.0).astype(jnp.bfloat16)
    acts[...] = jnp.zeros_like(acts)

    def send_terms(k):
        for j in range(1, PLANE):
            term_copy(k, j).start()

    def pass_grad(k):
        grad_copy(k).wait_recv()
        far_g[k] = (keep[k] + got_g[k, 1].astype(jnp.float32)).astype(jnp.bfloat16)
        far_copy(k).start()

    @pl.loop(0, chunks)
    def _(k):
        @pl.when(k + AHEAD < chunks)
        def _():
            pass_down(k + AHEAD)

        @pl.when(jnp.logical_not(carrier))
        def _():
            for j in range(1, layers):
                hand_down(k, j).wait_recv()

        downs = all_down[k].reshape(all_rank, width)
        term = dot(low[...], downs).astype(jnp.bfloat16).reshape(PLANE, block, width)
        terms[k] = term
        back[k, column] = terms[k, column]

        @pl.when(k >= HOLD)
        def _():
            send_terms(2 * (k - HOLD))
            send_terms(2 * (k - HOLD) + 1)

        for j in range(1, PLANE):
            token_copy(k, j).wait_recv()
        tokens = got_t[k].reshape(slots, width)
        grad[...] = dot(low_t[...], tokens).reshape(layers, rank, width)
        send_g[k, 0] = grad[pair].astype(jnp.bfloat16)
        send_g[k, 1] = grad[pair_far].astype(jnp.bfloat16)
        grad_copy(k).start()
        down_grad_ref[:, span(k)] = grad[layer]
        keep[k] = grad[far]
        acts[...] += lax.dot_general(downs, tokens, NT, preferred_element_type=jnp.float32)

        @pl.when(k >= LAG)
        def _():
            pass_grad(k - LAG)

    for k in range(2 * (chunks - HOLD), chunks):
        send_terms(k)

    acts_low = jnp.where(own((all_rank, slots), 1, 0), acts[...], 0.0).astype(jnp.bfloat16)
    keep_u[...] = dot(acts_low, got_c[...].reshape(slots, got_c.shape[2])).reshape(keep_u.shape)
    send_u[0] = keep_u[pair].astype(jnp.bfloat16)
    send_u[1] = keep_u[pair_far].astype(jnp.bfloat16)
    up_grad_copy().start()

    for k in range(chunks - LAG, chunks):
        pass_grad(k)
    up_grad_copy().wait_recv()
    far_u[...] = (keep_u[far] + got_u[1].astype(jnp.float32)).astype(jnp.bfloat16)
    up_far_copy().start()

    def row_out(k):
        return pltpu.make_async_copy(
            out_ref.at[:, span(k)], out_hbm.at[:, span(k)], out_sem.at[k]
        )

    def grad_out(k):
        return pltpu.make_async_copy(
            down_grad_ref.at[:, span(k)], down_grad_hbm.at[:, span(k)], grad_sem.at[k]
        )

    up_out = pltpu.make_async_copy(up_grad_ref, up_grad_hbm, up_out_sem)

    @pl.loop(0, chunks)
    def _(k):
        far_copy(k).wait_recv()
        down_grad_ref[:, span(k)] = (
            down_grad_ref[:, span(k)]
            + got_g[k, 0].astype(jnp.float32)
            + in_g[k].astype(jnp.float32)
        )
        grad_out(k).start()

    up_far_copy().wait_recv()
    up_grad_ref[...] = (
        keep_u[layer] + got_u[0].astype(jnp.float32) + in_u[...].astype(jnp.float32)
    )
    up_out.start()

    @pl.loop(0, chunks)
    def _(k):
        for j in range(1, PLANE):
            term_copy(k, j).wait_recv()
        returned = dot(unplace[...], back[k].reshape(slots, width))
        out_ref[:, span(k)] = (base[k] + returned).astype(jnp.bfloat16)
        row_out(k).start()

    up_out.wait()
    up_grad_copy().wait_send()
    up_far_copy().wait_send()
    for j in range(1, PLANE):
        value_copy(j).wait_send()

    @pl.when(carrier)
    def _():
        for j in range(1, layers):
            up_copy(j).wait_send()
            hand_up(j).wait_send()

    @pl.loop(0, chunks)
    def _(k):
        row_out(k).wait()
        grad_out(k).wait()
        grad_copy(k).wait_send()
        far_copy(k).wait_send()
        for j in range(1, PLANE):
            token_copy(k, j).wait_send()
            term_copy(k, j).wait_send()

        @pl.when(carrier)
        def _():
            for j in range(1, layers):
                down_copy(k, j).wait_send()
                hand_down(k, j).wait_send()


def fused(
    tokens, cotangent, frozen_value_weight, adapter_down_weight, adapter_up_weight, speaker_of_clip
):
    owners = lax.axis_size("owner")
    layers = owners // PLANE
    clip_count = speaker_of_clip.shape[0] // owners
    rows, model_width = tokens.shape
    value_width = cotangent.shape[1]
    clip_rows = rows // clip_count
    rank = adapter_down_weight.shape[1]
    chunks = 4
    width = model_width // chunks
    block = layers * CAP * clip_rows
    slots = PLANE * block
    half = jnp.bfloat16
    vmem = pl.BlockSpec(memory_space=pltpu.VMEM)
    anywhere = pl.BlockSpec(memory_space=pl.ANY)
    dma = pltpu.SemaphoreType.DMA
    out, down_grad, up_grad = pl.pallas_call(
        functools.partial(kernel, layers, clip_count, clip_rows, chunks),
        out_shape=(
            jax.ShapeDtypeStruct((rows, model_width), half),
            jax.ShapeDtypeStruct((rank, model_width), jnp.float32),
            jax.ShapeDtypeStruct((rank, value_width), jnp.float32),
        ),
        in_specs=[pl.BlockSpec(memory_space=pltpu.SMEM), anywhere, vmem, anywhere, vmem, anywhere],
        out_specs=(anywhere, anywhere, anywhere),
        scratch_shapes=[
            pltpu.VMEM((rows, model_width), half),
            pltpu.VMEM((rank, model_width), half),
            pltpu.VMEM((rows, model_width), half),
            pltpu.VMEM((rank, model_width), jnp.float32),
            pltpu.VMEM((rank, value_width), jnp.float32),
            pltpu.VMEM((model_width, value_width), half),
            pltpu.VMEM((slots, rows), half),
            pltpu.VMEM((rows, slots), half),
            pltpu.VMEM((chunks, PLANE, block, width), half),
            pltpu.VMEM((PLANE, block, value_width), half),
            pltpu.VMEM((chunks, PLANE, block, width), half),
            pltpu.VMEM((PLANE, block, value_width), half),
            pltpu.VMEM((chunks, layers, rank, width), half),
            pltpu.VMEM((layers, rank, value_width), half),
            pltpu.VMEM((slots, layers * rank), half),
            pltpu.VMEM((layers * rank, slots), half),
            pltpu.VMEM((layers * rank, slots), jnp.float32),
            pltpu.VMEM((chunks, PLANE, block, width), half),
            pltpu.VMEM((chunks, PLANE, block, width), half),
            pltpu.VMEM((layers, rank, width), jnp.float32),
            pltpu.VMEM((chunks, rank, width), jnp.float32),
            pltpu.VMEM((chunks, 2, rank, width), half),
            pltpu.VMEM((chunks, 2, rank, width), half),
            pltpu.VMEM((chunks, rank, width), half),
            pltpu.VMEM((chunks, rank, width), half),
            pltpu.VMEM((layers, rank, value_width), jnp.float32),
            pltpu.VMEM((2, rank, value_width), half),
            pltpu.VMEM((2, rank, value_width), half),
            pltpu.VMEM((rank, value_width), half),
            pltpu.VMEM((rank, value_width), half),
            pltpu.VMEM((chunks, rows, width), jnp.float32),
            dma((2,)),
            dma((chunks,)),
            dma((chunks,)),
            dma(()),
            dma(()),
            dma((2, chunks, PLANE)),
            dma((2, PLANE)),
            dma((2, chunks, layers)),
            dma((2, layers)),
            dma((2, chunks, PLANE)),
            dma((2, chunks)),
            dma((2, chunks)),
            dma((2, 1)),
            dma((2, 1)),
            dma((2, chunks, layers)),
            dma((2, layers)),
        ],
        compiler_params=pltpu.CompilerParams(
            collective_id=0, has_side_effects=True, vmem_limit_bytes=56 * 2**20
        ),
        cost_estimate=pl.CostEstimate(
            flops=8 * 10**9, bytes_accessed=16 * 2**20, transcendentals=0
        ),
    )(
        speaker_of_clip,
        tokens,
        cotangent,
        adapter_down_weight[0],
        adapter_up_weight[0],
        frozen_value_weight,
    )
    return out, down_grad[None], up_grad[None]


def solution(mesh):
    sizes = [mesh.shape[axis] for axis in ("groups", "owner", "tensor")]
    body = fused if sizes == [2, 16, 1] else shards
    return jax.shard_map(
        body,
        mesh=mesh,
        in_specs=(
            P(("groups", "owner"), "tensor"),
            P(("groups", "owner"), None),
            P("tensor", None),
            P("owner", None, "tensor"),
            P("owner", None, "tensor"),
            P("groups"),
        ),
        out_specs=(
            P(("groups", "owner"), "tensor"),
            P(("groups", "owner"), None, "tensor"),
            P(("groups", "owner"), None, "tensor"),
        ),
        check_vma=False,
    )
```

```python
import functools

import jax
import jax.numpy as jnp
from jax import lax
from jax.experimental import pallas as pl
from jax.experimental.pallas import tpu as pltpu
from jax.sharding import PartitionSpec as P

CAP = 2


def shards(
    tokens, cotangent, frozen_value_weight, adapter_down_weight, adapter_up_weight, speaker_of_clip
):
    owners = lax.axis_size("owner")
    my_index = lax.axis_index("owner")
    core_index = lax.axis_index("tensor")
    clip_count = speaker_of_clip.shape[0] // owners
    clip_rows = tokens.shape[0] // clip_count
    model_width_half = tokens.shape[1]
    value_width_half = adapter_up_weight.shape[2]
    slot_count = owners * CAP
    contract_last = (((1,), (1,)), ((), ()))
    contract_leading = (((0,), (0,)), ((), ()))
    my_clips = lax.dynamic_slice_in_dim(speaker_of_clip, my_index * clip_count, clip_count)
    clip_order = jnp.arange(clip_count)
    earlier = (my_clips[:, None] == my_clips[None, :]) & (clip_order[None, :] < clip_order[:, None])
    position = jnp.sum(earlier.astype(jnp.int32), axis=1)
    target = my_clips * CAP + position
    placing = (jnp.arange(slot_count)[:, None] == target[None, :]).astype(jnp.bfloat16)
    value_rows = lax.dynamic_slice_in_dim(
        cotangent, core_index * value_width_half, value_width_half, 1
    )
    send_tokens = jnp.dot(
        placing, tokens.reshape(clip_count, -1), preferred_element_type=jnp.float32
    )
    send_tokens = send_tokens.astype(jnp.bfloat16).reshape(
        owners, CAP * clip_rows, model_width_half
    )
    send_values = jnp.dot(
        placing, value_rows.reshape(clip_count, -1), preferred_element_type=jnp.float32
    )
    send_values = send_values.astype(jnp.bfloat16).reshape(
        owners, CAP * clip_rows, value_width_half
    )
    got_tokens, got_values = (
        lax.all_to_all(send_tokens, "owner", split_axis=0, concat_axis=0, tiled=True),
        lax.all_to_all(send_values, "owner", split_axis=0, concat_axis=0, tiled=True),
    )
    in_rows = got_tokens.reshape(-1, model_width_half)
    in_values = got_values.reshape(-1, value_width_half)
    down_gradient_local = adapter_down_weight[0]
    up_gradient_local = adapter_up_weight[0]
    acts_part = lax.dot_general(
        down_gradient_local, in_rows, contract_last, preferred_element_type=jnp.float32
    )
    back_part = lax.dot_general(
        up_gradient_local, in_values, contract_last, preferred_element_type=jnp.float32
    )
    acts_sum, back_sum = lax.psum((acts_part, back_part), "tensor")
    acts_low = acts_sum.astype(jnp.bfloat16)
    low_rank_gradient = back_sum.astype(jnp.bfloat16)
    down_grad = jnp.dot(low_rank_gradient, in_rows, preferred_element_type=jnp.float32)[None]
    up_grad = jnp.dot(acts_low, in_values, preferred_element_type=jnp.float32)[None]
    frozen_gradient = lax.dot_general(
        cotangent, frozen_value_weight, contract_last, preferred_element_type=jnp.float32
    )
    slot_terms = lax.dot_general(
        low_rank_gradient, down_gradient_local, contract_leading, preferred_element_type=jnp.float32
    )
    slot_terms = slot_terms.astype(jnp.bfloat16).reshape(owners, CAP * clip_rows, model_width_half)
    returned = lax.all_to_all(slot_terms, "owner", split_axis=0, concat_axis=0, tiled=True)
    adapter_gradient = lax.dot_general(
        placing,
        returned.reshape(slot_count, -1),
        contract_leading,
        preferred_element_type=jnp.float32,
    )
    adapter_gradient = adapter_gradient.reshape(-1, model_width_half)
    input_row_gradient = (frozen_gradient + adapter_gradient).astype(jnp.bfloat16)
    return (input_row_gradient, down_grad, up_grad)


PLANE = 4
AHEAD = 2
LAG = 1
HOLD = 2
MESH = pl.DeviceIdType.MESH
NT = (((1,), (1,)), ((), ()))


def dot(a, b):
    return jnp.dot(a, b, preferred_element_type=jnp.float32)


def slot_starts(clips_ref, first, clip_count, clip_rows, layers, block):
    speakers = [clips_ref[first + j] for j in range(clip_count)]
    starts = []
    for j in range(clip_count):
        position = jnp.int32(0)
        for i in range(j):
            position = position + jnp.where(speakers[i] == speakers[j], 1, 0)
        speaker = speakers[j]
        column = lax.rem(speaker, PLANE)
        layer = lax.div(speaker, PLANE)
        starts.append(column * block + layer * (CAP * clip_rows) + position * clip_rows)
    return starts


def placed_rows(starts, shape, dim, clip_rows):
    token = lax.broadcasted_iota(jnp.int32, shape, dim)
    clip = lax.div(token, clip_rows)
    target = lax.rem(token, clip_rows)
    for j, start in enumerate(starts):
        target = target + jnp.where(clip == j, start, 0)
    return target


def kernel(
    layers,
    clip_count,
    clip_rows,
    chunks,
    clips_ref,
    tokens_hbm,
    cotangent_ref,
    down_hbm,
    up_ref,
    frozen_ref,
    out_hbm,
    down_grad_hbm,
    up_grad_hbm,
    tokens_ref,
    down_ref,
    out_ref,
    down_grad_ref,
    up_grad_ref,
    frozen,
    place,
    unplace,
    send_t,
    send_c,
    got_t,
    got_c,
    all_down,
    all_up,
    low,
    low_t,
    acts,
    terms,
    back,
    grad,
    keep,
    send_g,
    got_g,
    far_g,
    in_g,
    keep_u,
    send_u,
    got_u,
    far_u,
    in_u,
    base,
    in_sem,
    out_sem,
    grad_sem,
    up_out_sem,
    frozen_sem,
    t_sem,
    c_sem,
    d_sem,
    u_sem,
    r_sem,
    g_sem,
    h_sem,
    v_sem,
    w_sem,
    x_sem,
    y_sem,
):
    me = lax.axis_index("owner")
    group = lax.axis_index("groups")
    column = me % PLANE
    layer = me // PLANE
    carrier = column % 2 == group
    pair = layer + 1 - 2 * (layer % 2)
    far = (layer + 2) % layers
    pair_far = (pair + 2) % layers
    rows = tokens_ref.shape[0]
    width = tokens_ref.shape[1] // chunks
    rank = down_ref.shape[0]
    block = layers * CAP * clip_rows
    slots = PLANE * block
    all_rank = layers * rank

    frozen_copy = pltpu.make_async_copy(frozen_ref, frozen, frozen_sem)
    tokens_in = pltpu.make_async_copy(tokens_hbm, tokens_ref, in_sem.at[0])
    down_in = pltpu.make_async_copy(down_hbm, down_ref, in_sem.at[1])
    tokens_in.start()
    down_in.start()

    def in_plane(j):
        return layer * PLANE + (column + j) % PLANE

    def in_line(j):
        return ((layer + j) % layers) * PLANE + column

    barrier = pltpu.get_barrier_semaphore()
    for j in range(1, PLANE):
        pl.semaphore_signal(barrier, inc=1, device_id={"owner": in_plane(j)}, device_id_type=MESH)
    for j in range(1, layers):
        pl.semaphore_signal(barrier, inc=1, device_id={"owner": in_line(j)}, device_id_type=MESH)
    across = {"groups": 1 - group, "owner": me}
    pl.semaphore_signal(barrier, inc=1, device_id=across, device_id_type=MESH)
    starts = slot_starts(clips_ref, me * clip_count, clip_count, clip_rows, layers, block)
    slot = lax.broadcasted_iota(jnp.int32, (slots, rows), 0)
    target = placed_rows(starts, (slots, rows), 1, clip_rows)
    place[...] = jnp.where(slot == target, 1.0, 0.0).astype(jnp.bfloat16)

    send_c[...] = (
        dot(place[...], cotangent_ref[...]).astype(jnp.bfloat16).reshape(send_c.shape)
    )
    pl.semaphore_wait(barrier, PLANE - 1 + layers - 1 + 1)

    def remote(src, dst, sems, at, owner):
        return pltpu.make_async_remote_copy(
            src_ref=src,
            dst_ref=dst,
            send_sem=sems.at[(0,) + at],
            recv_sem=sems.at[(1,) + at],
            device_id={"owner": owner},
            device_id_type=MESH,
        )

    def span(k):
        return pl.ds(pl.multiple_of(k * width, width), width)

    def up_copy(j):
        return remote(up_ref, all_up.at[layer], u_sem, (j,), in_line(j))

    def down_copy(k, j):
        return remote(
            down_ref.at[:, span(k)], all_down.at[k, layer], d_sem, (k, j), in_line(j)
        )

    def value_copy(j):
        return remote(
            send_c.at[(column + j) % PLANE], got_c.at[column], c_sem, (j,), in_plane(j)
        )

    def token_copy(k, j):
        return remote(
            send_t.at[k, (column + j) % PLANE], got_t.at[k, column], t_sem, (k, j), in_plane(j)
        )

    def term_copy(k, j):
        return remote(
            terms.at[k, (column + j) % PLANE], back.at[k, column], r_sem, (k, j), in_plane(j)
        )

    def grad_copy(k):
        return remote(send_g.at[k], got_g.at[k], g_sem, (k,), pair * PLANE + column)

    def far_copy(k):
        return remote(far_g.at[k], in_g.at[k], h_sem, (k,), far * PLANE + column)

    def up_grad_copy():
        return remote(send_u, got_u, v_sem, (0,), pair * PLANE + column)

    def up_far_copy():
        return remote(far_u, in_u, w_sem, (0,), far * PLANE + column)

    def hand(ref, sems, at):
        return pltpu.make_async_remote_copy(
            src_ref=ref,
            dst_ref=ref,
            send_sem=sems.at[(0,) + at],
            recv_sem=sems.at[(1,) + at],
            device_id=across,
            device_id_type=MESH,
        )

    def hand_down(k, j):
        return hand(all_down.at[k, (layer - j + layers) % layers], x_sem, (k, j))

    def hand_up(j):
        return hand(all_up.at[(layer - j + layers) % layers], y_sem, (j,))

    def pass_down(k):
        @pl.when(carrier)
        def _():
            for j in range(1, layers):
                down_copy(k, j).wait_recv()
                hand_down(k, j).start()

    @pl.when(carrier)
    def _():
        for j in range(1, layers):
            up_copy(j).start()

    for j in range(1, PLANE):
        value_copy(j).start()

    tokens_in.wait()
    down_in.wait()
    frozen_copy.start()

    @pl.loop(0, chunks)
    def _(k):
        @pl.when(carrier)
        def _():
            for j in range(1, layers):
                down_copy(k, j).start()

        placed = dot(place[...], tokens_ref[:, span(k)]).astype(jnp.bfloat16)
        send_t[k] = placed.reshape(PLANE, block, width)
        for j in range(1, PLANE):
            token_copy(k, j).start()
        got_t[k, column] = send_t[k, column]
        all_down[k, layer] = down_ref[:, span(k)]

    slot = lax.broadcasted_iota(jnp.int32, (rows, slots), 1)
    target = placed_rows(starts, (rows, slots), 0, clip_rows)
    unplace[...] = jnp.where(slot == target, 1.0, 0.0).astype(jnp.bfloat16)
    got_c[column] = send_c[column]
    all_up[layer] = up_ref[...]
    @pl.when(carrier)
    def _():
        for j in range(1, layers):
            up_copy(j).wait_recv()
            hand_up(j).start()

    for k in range(AHEAD):
        pass_down(k)

    @pl.when(jnp.logical_not(carrier))
    def _():
        for j in range(1, layers):
            hand_up(j).wait_recv()

    for j in range(1, PLANE):
        value_copy(j).wait_recv()

    def own(shape, slot_dim, rank_dim):
        slot_layer = lax.div(
            lax.rem(lax.broadcasted_iota(jnp.int32, shape, slot_dim), block), CAP * clip_rows
        )
        return slot_layer == lax.div(lax.broadcasted_iota(jnp.int32, shape, rank_dim), rank)

    values = got_c[...].reshape(slots, got_c.shape[2])
    ups = all_up[...].reshape(all_rank, all_up.shape[2])
    full = lax.dot_general(values, ups, NT, preferred_element_type=jnp.float32)
    low[...] = jnp.where(own((slots, all_rank), 0, 1), full, 0.0).astype(jnp.bfloat16)
    full = lax.dot_general(ups, values, NT, preferred_element_type=jnp.float32)
    low_t[...] = jnp.where(own((all_rank, slots), 1, 0), full, 0.0).astype(jnp.bfloat16)
    acts[...] = jnp.zeros_like(acts)

    def send_terms(k):
        for j in range(1, PLANE):
            term_copy(k, j).start()

    def pass_grad(k):
        grad_copy(k).wait_recv()
        far_g[k] = (keep[k] + got_g[k, 1].astype(jnp.float32)).astype(jnp.bfloat16)
        far_copy(k).start()

    @pl.loop(0, chunks)
    def _(k):
        @pl.when(k + AHEAD < chunks)
        def _():
            pass_down(k + AHEAD)

        @pl.when(jnp.logical_not(carrier))
        def _():
            for j in range(1, layers):
                hand_down(k, j).wait_recv()

        downs = all_down[k].reshape(all_rank, width)
        term = dot(low[...], downs).astype(jnp.bfloat16).reshape(PLANE, block, width)
        terms[k] = term
        back[k, column] = terms[k, column]

        @pl.when(k >= HOLD)
        def _():
            send_terms(2 * (k - HOLD))
            send_terms(2 * (k - HOLD) + 1)

        for j in range(1, PLANE):
            token_copy(k, j).wait_recv()
        tokens = got_t[k].reshape(slots, width)
        grad[...] = dot(low_t[...], tokens).reshape(layers, rank, width)
        send_g[k, 0] = grad[pair].astype(jnp.bfloat16)
        send_g[k, 1] = grad[pair_far].astype(jnp.bfloat16)
        grad_copy(k).start()
        down_grad_ref[:, span(k)] = grad[layer]
        keep[k] = grad[far]
        acts[...] += lax.dot_general(downs, tokens, NT, preferred_element_type=jnp.float32)

        @pl.when(k >= LAG)
        def _():
            pass_grad(k - LAG)

    for k in range(2 * (chunks - HOLD), chunks):
        send_terms(k)

    acts_low = jnp.where(own((all_rank, slots), 1, 0), acts[...], 0.0).astype(jnp.bfloat16)
    keep_u[...] = dot(acts_low, got_c[...].reshape(slots, got_c.shape[2])).reshape(keep_u.shape)
    send_u[0] = keep_u[pair].astype(jnp.bfloat16)
    send_u[1] = keep_u[pair_far].astype(jnp.bfloat16)
    up_grad_copy().start()

    frozen_copy.wait()

    @pl.loop(0, chunks)
    def _(k):
        base[k] = lax.dot_general(
            cotangent_ref[...],
            frozen[span(k), :],
            NT,
            preferred_element_type=jnp.float32,
        )

    for k in range(chunks - LAG, chunks):
        pass_grad(k)
    up_grad_copy().wait_recv()
    far_u[...] = (keep_u[far] + got_u[1].astype(jnp.float32)).astype(jnp.bfloat16)
    up_far_copy().start()

    def row_out(k):
        return pltpu.make_async_copy(
            out_ref.at[:, span(k)], out_hbm.at[:, span(k)], out_sem.at[k]
        )

    def grad_out(k):
        return pltpu.make_async_copy(
            down_grad_ref.at[:, span(k)], down_grad_hbm.at[:, span(k)], grad_sem.at[k]
        )

    up_out = pltpu.make_async_copy(up_grad_ref, up_grad_hbm, up_out_sem)

    @pl.loop(0, chunks)
    def _(k):
        far_copy(k).wait_recv()
        down_grad_ref[:, span(k)] = (
            down_grad_ref[:, span(k)]
            + got_g[k, 0].astype(jnp.float32)
            + in_g[k].astype(jnp.float32)
        )
        grad_out(k).start()

    up_far_copy().wait_recv()
    up_grad_ref[...] = (
        keep_u[layer] + got_u[0].astype(jnp.float32) + in_u[...].astype(jnp.float32)
    )
    up_out.start()

    @pl.loop(0, chunks)
    def _(k):
        for j in range(1, PLANE):
            term_copy(k, j).wait_recv()
        returned = dot(unplace[...], back[k].reshape(slots, width))
        out_ref[:, span(k)] = (base[k] + returned).astype(jnp.bfloat16)
        row_out(k).start()

    up_out.wait()
    up_grad_copy().wait_send()
    up_far_copy().wait_send()
    for j in range(1, PLANE):
        value_copy(j).wait_send()

    @pl.when(carrier)
    def _():
        for j in range(1, layers):
            up_copy(j).wait_send()
            hand_up(j).wait_send()

    @pl.loop(0, chunks)
    def _(k):
        row_out(k).wait()
        grad_out(k).wait()
        grad_copy(k).wait_send()
        far_copy(k).wait_send()
        for j in range(1, PLANE):
            token_copy(k, j).wait_send()
            term_copy(k, j).wait_send()

        @pl.when(carrier)
        def _():
            for j in range(1, layers):
                down_copy(k, j).wait_send()
                hand_down(k, j).wait_send()


def fused(
    tokens, cotangent, frozen_value_weight, adapter_down_weight, adapter_up_weight, speaker_of_clip
):
    owners = lax.axis_size("owner")
    layers = owners // PLANE
    clip_count = speaker_of_clip.shape[0] // owners
    rows, model_width = tokens.shape
    value_width = cotangent.shape[1]
    clip_rows = rows // clip_count
    rank = adapter_down_weight.shape[1]
    chunks = 4
    width = model_width // chunks
    block = layers * CAP * clip_rows
    slots = PLANE * block
    half = jnp.bfloat16
    vmem = pl.BlockSpec(memory_space=pltpu.VMEM)
    anywhere = pl.BlockSpec(memory_space=pl.ANY)
    dma = pltpu.SemaphoreType.DMA
    out, down_grad, up_grad = pl.pallas_call(
        functools.partial(kernel, layers, clip_count, clip_rows, chunks),
        out_shape=(
            jax.ShapeDtypeStruct((rows, model_width), half),
            jax.ShapeDtypeStruct((rank, model_width), jnp.float32),
            jax.ShapeDtypeStruct((rank, value_width), jnp.float32),
        ),
        in_specs=[pl.BlockSpec(memory_space=pltpu.SMEM), anywhere, vmem, anywhere, vmem, anywhere],
        out_specs=(anywhere, anywhere, anywhere),
        scratch_shapes=[
            pltpu.VMEM((rows, model_width), half),
            pltpu.VMEM((rank, model_width), half),
            pltpu.VMEM((rows, model_width), half),
            pltpu.VMEM((rank, model_width), jnp.float32),
            pltpu.VMEM((rank, value_width), jnp.float32),
            pltpu.VMEM((model_width, value_width), half),
            pltpu.VMEM((slots, rows), half),
            pltpu.VMEM((rows, slots), half),
            pltpu.VMEM((chunks, PLANE, block, width), half),
            pltpu.VMEM((PLANE, block, value_width), half),
            pltpu.VMEM((chunks, PLANE, block, width), half),
            pltpu.VMEM((PLANE, block, value_width), half),
            pltpu.VMEM((chunks, layers, rank, width), half),
            pltpu.VMEM((layers, rank, value_width), half),
            pltpu.VMEM((slots, layers * rank), half),
            pltpu.VMEM((layers * rank, slots), half),
            pltpu.VMEM((layers * rank, slots), jnp.float32),
            pltpu.VMEM((chunks, PLANE, block, width), half),
            pltpu.VMEM((chunks, PLANE, block, width), half),
            pltpu.VMEM((layers, rank, width), jnp.float32),
            pltpu.VMEM((chunks, rank, width), jnp.float32),
            pltpu.VMEM((chunks, 2, rank, width), half),
            pltpu.VMEM((chunks, 2, rank, width), half),
            pltpu.VMEM((chunks, rank, width), half),
            pltpu.VMEM((chunks, rank, width), half),
            pltpu.VMEM((layers, rank, value_width), jnp.float32),
            pltpu.VMEM((2, rank, value_width), half),
            pltpu.VMEM((2, rank, value_width), half),
            pltpu.VMEM((rank, value_width), half),
            pltpu.VMEM((rank, value_width), half),
            pltpu.VMEM((chunks, rows, width), jnp.float32),
            dma((2,)),
            dma((chunks,)),
            dma((chunks,)),
            dma(()),
            dma(()),
            dma((2, chunks, PLANE)),
            dma((2, PLANE)),
            dma((2, chunks, layers)),
            dma((2, layers)),
            dma((2, chunks, PLANE)),
            dma((2, chunks)),
            dma((2, chunks)),
            dma((2, 1)),
            dma((2, 1)),
            dma((2, chunks, layers)),
            dma((2, layers)),
        ],
        compiler_params=pltpu.CompilerParams(
            collective_id=0, has_side_effects=True, vmem_limit_bytes=56 * 2**20
        ),
        cost_estimate=pl.CostEstimate(
            flops=8 * 10**9, bytes_accessed=16 * 2**20, transcendentals=0
        ),
    )(
        speaker_of_clip,
        tokens,
        cotangent,
        adapter_down_weight[0],
        adapter_up_weight[0],
        frozen_value_weight,
    )
    return out, down_grad[None], up_grad[None]


def solution(mesh):
    sizes = [mesh.shape[axis] for axis in ("groups", "owner", "tensor")]
    body = fused if sizes == [2, 16, 1] else shards
    return jax.shard_map(
        body,
        mesh=mesh,
        in_specs=(
            P(("groups", "owner"), "tensor"),
            P(("groups", "owner"), None),
            P("tensor", None),
            P("owner", None, "tensor"),
            P("owner", None, "tensor"),
            P("groups"),
        ),
        out_specs=(
            P(("groups", "owner"), "tensor"),
            P(("groups", "owner"), None, "tensor"),
            P(("groups", "owner"), None, "tensor"),
        ),
        check_vma=False,
    )
```
